32 devices in a mesh: groups: 1, ctx: 16 (over z, y, x), tp: 2 (over core).
Axes of the slice: x: 2, y: 2, z: 4, core: 2. Of those that a mesh axis runs over, the one named last changes fastest.
Arguments:
- queries: bfloat16 [4, 32, 64, 128], P('groups', 'ctx', 'tp'), may hold values from -100 to 100
- cand_keys: bfloat16 [4, 32, 8, 128], P('groups', 'ctx', 'tp'), may hold values from -4 to 4
- candidate_values: bfloat16 [4, 32, 8, 128], P('groups', 'ctx', 'tp'), may hold values from -5 to 5
- cached_prompt_keys: bfloat16 [256, 128, 8, 128], P(('groups', 'ctx'), None, 'tp'), may hold values from -4 to 4
- cached_prompt_values: bfloat16 [256, 128, 8, 128], P(('groups', 'ctx'), None, 'tp'), may hold values from -5 to 5
- block_lists: int32 [4, 128], P('groups'), may hold values from 0 to 255, as said below
- out_weight: bfloat16 [8192, 8192], P('tp', 'ctx'), may hold values from -0.0625 to 0.0625
Outputs:
- verified: bfloat16 [4, 32, 8192], P('groups', 'tp', 'ctx')
The draws below stay inside these ranges and needn't reach their ends.
Inputs may be any that keep to these rules, and one draw needn't show every extreme that they name: `block_lists`: each row holds 128 distinct block numbers in increasing order; among blocks 16 * c to 16 * (c + 1) - 1 a row has at most 16 entries, exactly 16 for some c in every row; all rows together have at most 40 entries in one such range, exactly 40 in some.
All inputs are finite; a program needn't handle non-finite values.
Results may differ from the reference program's by a relative error of at most 0.022.
Values may be sent and summed in bfloat16 or wider, within the bound.
No kernel may reach another device: no remote copies, remote signals or barrier semaphores. Data moves between devices by JAX's collectives and lax.ppermute only.
A program may use at most 128 MiB of HBM per device.

```python
import jax
import jax.numpy as jnp
from jax import lax

D = 8192
QUERY_HEADS = 64
KEY_VALUE_HEADS = 8
HEAD_WIDTH = 128
PROMPT_BLOCK = 128
READ_BLOCKS = 128
CANDIDATE_COUNT = 4
BLK_DEV = 16
PROMPT_BLOCKS = 256
CANDIDATE_LENGTH = 32


def paired_draw(key):
    base = jax.random.fold_in(key, 7)
    key_one, random_key_second = jax.random.split(base, 2)
    candidate_own_keys = jnp.clip(jax.random.normal(random_key_second, (CANDIDATE_COUNT, CANDIDATE_LENGTH, KEY_VALUE_HEADS, HEAD_WIDTH), jnp.float32), -4.0, 4.0)
    query_matrix = jnp.clip(jax.random.normal(key_one, (CANDIDATE_COUNT, CANDIDATE_LENGTH, QUERY_HEADS, HEAD_WIDTH), jnp.float32), -4.0, 4.0)
    return (query_matrix, candidate_own_keys)


def draw_queries(key, part):
    return paired_draw(key)[0].astype(jnp.bfloat16)


def draw_cand_keys(key, part):
    return paired_draw(key)[1].astype(jnp.bfloat16)


def draw_block_lists(key, part):
    ranges = PROMPT_BLOCKS // BLK_DEV
    most = min(BLK_DEV, 4 * READ_BLOCKS // ranges)
    second = most // 2
    base = jax.random.fold_in(key, 11)
    busiest = jax.random.permutation(jax.random.fold_in(base, 1), ranges)[:CANDIDATE_COUNT]

    def candidate(index):
        own_key = jax.random.fold_in(base, 100 + index)
        key_one, random_key_second = jax.random.split(own_key)
        device = jnp.arange(ranges)
        is_busy = device == busiest[index]
        forced = (device == busiest[0]) & (index > 0)
        remaining = READ_BLOCKS - most - jnp.where(index > 0, second, 0)
        scores = jax.random.permutation(key_one, ranges * second).reshape(ranges, second)
        eligible = jnp.logical_not(is_busy | forced)
        scores = jnp.where(eligible[:, None], scores, ranges * second + 1)
        ranking = jnp.argsort(jnp.argsort(scores.reshape(-1))).reshape(ranges, second)
        chosen = ranking < remaining
        counts = jnp.where(is_busy, most, jnp.where(forced, second, jnp.sum(chosen.astype(jnp.int32), axis=1)))
        orders = jax.vmap(lambda sub: jax.random.permutation(sub, BLK_DEV))(jax.random.split(random_key_second, ranges))[:, :most]
        blocks = device[:, None] * BLK_DEV + orders
        slot = jnp.arange(most)
        marked = jnp.where(slot[None, :] < counts[:, None], blocks, PROMPT_BLOCKS + 1)
        return jnp.sort(marked.reshape(-1))[:READ_BLOCKS].astype(jnp.int32)
    return jax.vmap(candidate)(jnp.arange(CANDIDATE_COUNT))


def block_levels(rng, dims, pieces, smallest, largest):
    gain, own = 1.0, jax.random.fold_in(rng, 6)
    for dim, blocks in pieces:
        heights = jnp.exp(jax.random.uniform(jax.random.fold_in(own, dim), (blocks,), jnp.float32, smallest / len(pieces), largest / len(pieces)))
        gain = gain * jnp.repeat(heights, dims[dim] // blocks).reshape([-1 if axis == dim else 1 for axis in range(len(dims))])
    return gain


def scatter_about(key, extent, spread, limit, pieces=(), kind=jnp.bfloat16):
    result = spread * jax.random.normal(key, extent, jnp.float32)
    if pieces:
        result = result * block_levels(key, extent, pieces, -0.22, 0.18)
    return jnp.clip(result, -limit, limit).astype(kind)


def setup_inputs(seed: int = 0, part: int = 0) -> dict:
    streams_of = jax.random.split(jax.random.key(seed), 8)
    own_keys = jax.random.split(jax.random.fold_in(streams_of[7], part), 8)
    queries = draw_queries(jax.random.fold_in(jax.random.fold_in(streams_of[7], part), 71), part)
    cand_keys = draw_cand_keys(jax.random.fold_in(jax.random.fold_in(streams_of[7], part), 71), part)
    candidate_values = scatter_about(own_keys[2], (CANDIDATE_COUNT, CANDIDATE_LENGTH, KEY_VALUE_HEADS, HEAD_WIDTH), 1.0, 5.0, ((1, 16), (2, 2)))
    cached_prompt_keys = scatter_about(own_keys[3], (PROMPT_BLOCKS, PROMPT_BLOCK, KEY_VALUE_HEADS, HEAD_WIDTH), 1.0, 4.0, ((0, 16), (2, 2)))
    cached_prompt_values = scatter_about(own_keys[4], (PROMPT_BLOCKS, PROMPT_BLOCK, KEY_VALUE_HEADS, HEAD_WIDTH), 1.0, 5.0, ((0, 16), (2, 2)))
    block_lists = draw_block_lists(jax.random.fold_in(jax.random.fold_in(streams_of[7], part), 71), part)
    out_weight = scatter_about(streams_of[6], (QUERY_HEADS * HEAD_WIDTH, D), (QUERY_HEADS * HEAD_WIDTH) ** -0.5, 0.0625, ((0, 2), (1, 16)))
    return dict(queries=queries, cand_keys=cand_keys, candidate_values=candidate_values, cached_prompt_keys=cached_prompt_keys, cached_prompt_values=cached_prompt_values, block_lists=block_lists, out_weight=out_weight)


def reference(queries, cand_keys, candidate_values, cached_prompt_keys, cached_prompt_values, block_lists, out_weight):
    query_group_width = QUERY_HEADS // KEY_VALUE_HEADS
    factor = HEAD_WIDTH ** -0.5
    position = jnp.arange(CANDIDATE_LENGTH)
    causal = position[None, :] <= position[:, None]
    visible = jnp.concatenate([jnp.ones((CANDIDATE_LENGTH, READ_BLOCKS * PROMPT_BLOCK), dtype=bool), causal], axis=1)

    def candidate(inputs):
        query_matrix, candidate_own_keys, own_values, listed_blocks = inputs
        gathered_keys = jnp.take(cached_prompt_keys, listed_blocks, axis=0).reshape(READ_BLOCKS * PROMPT_BLOCK, KEY_VALUE_HEADS, HEAD_WIDTH)
        gathered_values = jnp.take(cached_prompt_values, listed_blocks, axis=0).reshape(READ_BLOCKS * PROMPT_BLOCK, KEY_VALUE_HEADS, HEAD_WIDTH)
        all_keys = jnp.concatenate([gathered_keys, candidate_own_keys], axis=0)
        all_values = jnp.concatenate([gathered_values, own_values], axis=0)
        grouped_queries = query_matrix.reshape(CANDIDATE_LENGTH, KEY_VALUE_HEADS, query_group_width, HEAD_WIDTH)

        def kv_head(parts):
            head_queries, head_keys, head_values = parts
            scores = jnp.einsum('ngd,md->gnm', head_queries.astype(jnp.float32), head_keys.astype(jnp.float32)) * factor
            scores = jnp.where(visible[None], scores, -1e30)
            maxima = jnp.max(scores, axis=-1, keepdims=True)
            expon = jnp.where(visible[None], jnp.exp(scores - maxima), 0.0)
            denominator = jnp.sum(expon, axis=-1)
            rounded = lax.optimization_barrier(expon.astype(jnp.bfloat16)).astype(jnp.float32)
            numerator = jnp.einsum('gnm,md->ngd', rounded, head_values.astype(jnp.float32))
            return numerator / jnp.transpose(denominator)[:, :, None]

        heads_out = lax.map(kv_head, (jnp.transpose(grouped_queries, (1, 0, 2, 3)), jnp.transpose(all_keys, (1, 0, 2)), jnp.transpose(all_values, (1, 0, 2))))
        return jnp.transpose(heads_out, (1, 0, 2, 3)).reshape(CANDIDATE_LENGTH, QUERY_HEADS * HEAD_WIDTH).astype(jnp.bfloat16)

    attention = lax.map(candidate, (queries, cand_keys, candidate_values, block_lists))
    product = jnp.dot(attention.reshape(CANDIDATE_COUNT * CANDIDATE_LENGTH, QUERY_HEADS * HEAD_WIDTH), out_weight, preferred_element_type=jnp.float32)
    return product.astype(jnp.bfloat16).reshape(CANDIDATE_COUNT, CANDIDATE_LENGTH, D)
```

```python
import functools
import math

import jax
import jax.numpy as jnp
from jax import lax
from jax.experimental import pallas as pl
from jax.experimental.pallas import tpu as pltpu
from jax.sharding import PartitionSpec as P

NEGATIVE = -1e30
POSITIVE = 1e30
STATS = 3
OWN_ROWS = 16
GROUP = 4
LIMIT = 48 * 1024 * 1024

NT = (((1,), (1,)), ((), ()))
TN = (((0,), (0,)), ((), ()))


def whole(space=pltpu.VMEM):
    return pl.BlockSpec(memory_space=space)


def in_bf16(value):
    return value.astype(jnp.bfloat16).astype(jnp.float32)


def stat_rows(units):
    return -(-units * STATS // 16) * 16


class Sizes:
    def __init__(self, ranges, queries, cached, kv):
        self.n = ranges
        self.cand, self.toks, self.heads, self.width = queries
        self.kv = kv
        self.group = self.heads // kv
        self.blocks, self.block_tokens = cached[0], cached[1]
        self.lines = ranges // kv
        self.row_groups = self.lines // self.cand
        self.tokens = self.toks * ranges
        self.group_tokens = self.tokens // self.row_groups
        self.rows = self.group_tokens * self.group
        if kv != 4 or self.row_groups * self.cand * kv != ranges:
            raise ValueError("shape")


def place(size, line, first, second):
    me, core = lax.axis_index("ctx"), lax.axis_index("tp")
    other = (me // size.kv) ^ line
    return other * size.kv + ((me % size.kv) ^ (first * (1 + core)) ^ (second * (2 - core)))


def hop(size, value, stage):
    pairs = []
    cores = lax.axis_size("tp")
    for c in range(size.n):
        for core in range(cores):
            if stage == "first":
                other = c ^ (1 + core)
            elif stage == "second":
                other = c ^ (2 - core)
            else:
                other = c ^ (stage * size.kv)
            pairs.append((c * cores + core, other * cores + core))
    return lax.ppermute(value, ("ctx", "tp"), pairs)


def gather_lines(size, value):
    return jnp.stack([value] + [hop(size, value, k) for k in range(1, size.lines)])


def attention_kernel(
    size, first, lists, counts, q0, q1, q2, q3, keys, values, own_keys, own_values, out, rows, acc, stats
):
    units = 2 * size.lines
    scale = size.width ** (-0.5) * math.log2(math.e)
    me = lax.axis_index("ctx")
    for index, ref in enumerate((q0, q1, q2, q3)):
        for line in range(size.lines):
            chip = place(size, line, index % 2, index // 2)
            for j in range(size.cand):
                parts = [ref[line, j, t].astype(jnp.float32) for t in range(size.toks)]
                for kv in range(size.kv):
                    cut = [p[kv * size.group : (kv + 1) * size.group] for p in parts]
                    rows[j, kv, chip] = jnp.concatenate(cut).astype(jnp.bfloat16)
    chip_rows = size.toks * size.group
    chips = size.rows // chip_rows

    def one(step, carry):
        line = step
        j, part = line % size.cand, line // size.cand
        count = counts[j]
        matrices, held = [], []
        token = lax.broadcasted_iota(jnp.int32, (OWN_ROWS, size.rows), 1) // size.group
        token = token + part * size.group_tokens
        own = lax.broadcasted_iota(jnp.int32, (OWN_ROWS, size.rows), 0)
        seen = (own < size.toks) & (own + me * size.toks <= token)
        heads = [place(size, 0, first, second) % size.kv for second in range(2)]
        for second in range(2):
            q = rows[j, heads[second], pl.ds(part * chips, chips)].reshape(size.rows, size.width)
            matrices.append(q)
            s = lax.dot_general(
                own_keys[j, heads[second]], q, NT, preferred_element_type=jnp.float32
            )
            s = jnp.where(seen, s * scale, NEGATIVE)
            m = in_bf16(jnp.max(s, axis=0, keepdims=True))
            p = jnp.where(seen, jnp.exp2(s - m), 0.0)
            acc[second] = lax.dot_general(
                own_values[j, heads[second]],
                p.astype(jnp.bfloat16),
                TN,
                preferred_element_type=jnp.float32,
            )
            held += [m, jnp.sum(p, axis=0, keepdims=True)]

        def over(g, held):
            held = list(held)
            for second in range(2):
                m, l = held[2 * second], held[2 * second + 1]
                head, q = heads[second], matrices[second]
                scores, tops, live, cut = [], [], [], []
                for b in range(GROUP):
                    slot = g * GROUP + b
                    block = lists[j, slot]
                    alive = slot < count
                    s = lax.dot_general(
                        keys[head, block], q, NT, preferred_element_type=jnp.float32
                    )
                    top = jnp.max(s, axis=0, keepdims=True) * scale
                    scores.append(s)
                    live.append(alive)
                    tops.append(jnp.where(alive, top, NEGATIVE))
                    cut.append(values[head, block])
                top = functools.reduce(jnp.maximum, tops)
                high = jnp.maximum(m, in_bf16(top))
                fade = jnp.exp2(m - high)
                weights = []
                total = l * fade
                for b in range(GROUP):
                    shift = jnp.where(live[b], high, POSITIVE)
                    p = jnp.exp2(scores[b] * scale - shift)
                    total = total + jnp.sum(p, axis=0, keepdims=True)
                    weights.append(p.astype(jnp.bfloat16))
                acc[second] = acc[second] * fade + jnp.dot(
                    jnp.concatenate(cut, axis=1),
                    jnp.concatenate(weights, axis=0),
                    preferred_element_type=jnp.float32,
                )
                held[2 * second], held[2 * second + 1] = high, total
            return tuple(held)

        held = lax.fori_loop(0, (count + GROUP - 1) // GROUP, over, tuple(held))
        for second in range(2):
            unit = second * size.lines + line
            at = pl.multiple_of(unit * size.width, size.width)
            out[pl.ds(at, size.width), :] = acc[second].astype(jnp.bfloat16)
            m, l = held[2 * second], held[2 * second + 1]
            whole_l = in_bf16(l)
            stats[pl.ds(unit, 1), :] = m
            stats[pl.ds(units + unit, 1), :] = whole_l
            stats[pl.ds(2 * units + unit, 1), :] = l - whole_l
        return carry

    stats[...] = jnp.zeros_like(stats)
    lax.fori_loop(0, size.lines, one, 0)
    out[pl.ds(units * size.width, stat_rows(units)), :] = stats[...].astype(jnp.bfloat16)


def attention_part(size, first, lists, counts, gathered, keys, values, own_keys, own_values):
    units = 2 * size.lines
    length = units * size.width + stat_rows(units)
    return pl.pallas_call(
        functools.partial(attention_kernel, size, first),
        out_shape=jax.ShapeDtypeStruct((length, size.rows), jnp.bfloat16),
        in_specs=[whole(pltpu.SMEM)] * 2 + [whole()] * 8,
        out_specs=whole(),
        scratch_shapes=[
            pltpu.VMEM(
                (size.cand, size.kv, size.n, size.toks * size.group, size.width), jnp.bfloat16
            ),
            pltpu.VMEM((2, size.width, size.rows), jnp.float32),
            pltpu.VMEM((stat_rows(units), size.rows), jnp.float32),
        ],
        compiler_params=pltpu.CompilerParams(vmem_limit_bytes=LIMIT),
        name="attention",
    )(lists, counts, *gathered, keys, values, own_keys, own_values)


def merge_units(size, parts, unit_lists, units_of):
    stats = []
    for ref, units, unit in zip(parts, units_of, unit_lists):
        at = units * size.width
        block = ref[pl.ds(at, stat_rows(units)), :].astype(jnp.float32)
        m = block[unit : unit + 1]
        l = block[units + unit : units + unit + 1] + block[2 * units + unit : 2 * units + unit + 1]
        stats.append((m, l))
    high = functools.reduce(jnp.maximum, [m for m, _ in stats])
    fades = [jnp.exp2(m - high) for m, _ in stats]
    total = functools.reduce(jnp.add, [l * f for (_, l), f in zip(stats, fades)])
    sums = None
    for ref, unit, fade in zip(parts, unit_lists, fades):
        value = ref[pl.ds(unit * size.width, size.width), :].astype(jnp.float32) * fade
        sums = value if sums is None else sums + value
    return sums, high, total


def merge_kernel(size, start, units, units_in, mine, theirs, out):
    highs, totals = [], []
    for unit in range(units):
        sums, high, total = merge_units(size, (mine, theirs), (start + unit,) * 2, (units_in,) * 2)
        out[pl.ds(unit * size.width, size.width), :] = sums.astype(jnp.bfloat16)
        highs.append(high)
        totals.append(total)
    lengths = [in_bf16(t) for t in totals]
    rows = highs + lengths + [t - l for t, l in zip(totals, lengths)]
    left = stat_rows(units) - len(rows)
    if left:
        rows.append(jnp.zeros((left, size.rows), jnp.float32))
    out[pl.ds(units * size.width, stat_rows(units)), :] = jnp.concatenate(rows).astype(jnp.bfloat16)


def merge(size, start, units, units_in, mine, theirs):
    length = units * size.width + stat_rows(units)
    return pl.pallas_call(
        functools.partial(merge_kernel, size, start, units, units_in),
        out_shape=jax.ShapeDtypeStruct((length, size.rows), jnp.bfloat16),
        in_specs=[whole()] * 2,
        out_specs=whole(),
        compiler_params=pltpu.CompilerParams(vmem_limit_bytes=LIMIT),
        name="merge",
    )(mine, theirs)


def split_kernel(size, mine, theirs, own, *outs):
    here = lax.axis_index("ctx") // size.kv
    lines = size.lines
    parts = []
    for unit in range(lines):
        sums, high, total = merge_units(size, (mine, theirs), (unit, unit), (lines, lines))
        length = in_bf16(total)
        tail = jnp.concatenate(
            [high, length, total - length, jnp.zeros((16 - STATS, size.rows), jnp.float32)]
        )
        parts.append((sums.astype(jnp.bfloat16), tail.astype(jnp.bfloat16)))
    for line, out in enumerate((own,) + outs):
        for unit in range(lines):

            @pl.when((here ^ line) == unit)
            def _():
                out[: size.width, :] = parts[unit][0]
                out[size.width :, :] = parts[unit][1]


def split_merge(size, mine, theirs):
    shape = jax.ShapeDtypeStruct((size.width + 16, size.rows), jnp.bfloat16)
    return pl.pallas_call(
        functools.partial(split_kernel, size),
        out_shape=[shape] * size.lines,
        in_specs=[whole()] * 2,
        out_specs=[whole()] * size.lines,
        compiler_params=pltpu.CompilerParams(vmem_limit_bytes=LIMIT),
        name="split",
    )(mine, theirs)


def finish_kernel(size, *refs):
    parts, out, turned = refs[:-2], refs[-2], refs[-1]
    count = len(parts)
    sums, _, total = merge_units(size, parts, (0,) * count, (1,) * count)
    turned[...] = (sums / total).T
    for g in range(size.group):
        piece = turned[pl.ds(g, size.group_tokens, stride=size.group), :]
        out[pl.ds(g * size.group_tokens, size.group_tokens), :] = piece.astype(jnp.bfloat16)


def finish(size, parts):
    return pl.pallas_call(
        functools.partial(finish_kernel, size),
        out_shape=jax.ShapeDtypeStruct((size.rows, size.width), jnp.bfloat16),
        in_specs=[whole()] * len(parts),
        out_specs=whole(),
        scratch_shapes=[pltpu.VMEM((size.rows, size.width), jnp.float32)],
        compiler_params=pltpu.CompilerParams(vmem_limit_bytes=LIMIT),
        name="finish",
    )(*parts)


def project_kernel(size, a0, a1, a2, a3, weight, kept, sent, whole_rows, product):
    core = lax.axis_index("tp")
    for index, ref in enumerate((a0, a1, a2, a3)):
        for line in range(size.lines):
            chip = place(size, line, index % 2, index // 2)
            kv, other = chip % size.kv, chip // size.kv
            j, part = other % size.cand, other // size.cand
            at = pl.multiple_of(j * size.tokens + part * size.group_tokens, size.group_tokens)
            for g in range(size.group):
                piece = ref[line, pl.ds(g * size.group_tokens, size.group_tokens), :]
                whole_rows[kv * size.group + g, pl.ds(at, size.group_tokens), :] = piece
    total = None
    for h in range(0, size.heads, 2):
        pair = jnp.concatenate([whole_rows[h], whole_rows[h + 1]], axis=1)
        term = jnp.dot(
            pair,
            weight[pl.ds(h * size.width, 2 * size.width), :],
            preferred_element_type=jnp.float32,
        )
        total = term if total is None else total + term
    product[...] = total
    half = size.tokens // 2
    for j in range(size.cand):
        near = pl.multiple_of(j * size.tokens + core * half, half)
        far = pl.multiple_of(j * size.tokens + (1 - core) * half, half)
        kept[j] = product[pl.ds(near, half), :]
        sent[j] = product[pl.ds(far, half), :].astype(jnp.bfloat16)


def project(size, gathered, weight):
    columns = weight.shape[1]
    shape = (size.cand, size.tokens // 2, columns)
    return pl.pallas_call(
        functools.partial(project_kernel, size),
        out_shape=[
            jax.ShapeDtypeStruct(shape, jnp.float32),
            jax.ShapeDtypeStruct(shape, jnp.bfloat16),
        ],
        in_specs=[whole()] * 5,
        out_specs=[whole()] * 2,
        scratch_shapes=[
            pltpu.VMEM((size.heads, size.cand * size.tokens, size.width), jnp.bfloat16),
            pltpu.VMEM((size.cand * size.tokens, columns), jnp.float32),
        ],
        compiler_params=pltpu.CompilerParams(vmem_limit_bytes=LIMIT),
        name="project",
    )(*gathered, weight)


def gather_all(size, value):
    a0 = gather_lines(size, value)
    a1 = hop(size, a0, "first")
    a2 = hop(size, a0, "second")
    a3 = hop(size, a1, "second")
    return a0, a1, a2, a3


def listed_here(size, block_lists):
    lowest = lax.axis_index("ctx") * size.blocks
    local = block_lists - lowest
    below = jnp.sum((local < 0).astype(jnp.int32), axis=1)
    inside = jnp.sum((local < size.blocks).astype(jnp.int32), axis=1) - below
    slots = jnp.arange(-(-size.blocks // GROUP) * GROUP)
    entry = jnp.arange(block_lists.shape[1])
    hit = entry[None, None, :] == (below[:, None] + slots[None, :])[:, :, None]
    hit = hit & (slots[None, :] < inside[:, None])[:, :, None]
    return jnp.sum(jnp.where(hit, local[:, None, :], 0), axis=2), inside


def on_device(
    queries,
    cand_keys,
    candidate_values,
    cached_prompt_keys,
    cached_prompt_values,
    block_lists,
    out_weight,
):
    size = Sizes(
        lax.axis_size("ctx"), queries.shape, cached_prompt_keys.shape, cand_keys.shape[2]
    )
    gathered = gather_all(size, queries)
    lists, counts = listed_here(size, block_lists)
    keys = jnp.transpose(cached_prompt_keys, (2, 0, 1, 3))
    values = jnp.transpose(cached_prompt_values, (2, 0, 3, 1))
    room = ((0, 0), (0, 0), (0, OWN_ROWS - size.toks), (0, 0))
    own_keys = jnp.pad(jnp.transpose(cand_keys, (0, 2, 1, 3)), room)
    own_values = jnp.pad(jnp.transpose(candidate_values, (0, 2, 1, 3)), room)
    shared = (lists, counts, gathered, keys, values, own_keys, own_values)
    away = attention_part(size, 1, *shared)
    away = hop(size, away, "first")
    mine = attention_part(size, 0, *shared)
    lines = size.lines
    leaves = merge(size, lines, lines, 2 * lines, mine, away)
    leaves = hop(size, leaves, "second")
    stays = merge(size, 0, lines, 2 * lines, mine, away)
    parts = split_merge(size, stays, leaves)
    parts = [parts[0]] + [hop(size, parts[k], k) for k in range(1, lines)]
    attention = finish(size, parts)
    kept, sent = project(size, gather_all(size, attention), out_weight)
    cores = lax.axis_size("tp")
    sent = lax.ppermute(sent, "tp", [(i, cores - 1 - i) for i in range(cores)])
    return (kept + sent.astype(jnp.float32)).astype(jnp.bfloat16)


def solution(mesh):
    placed = (
        P("groups", "ctx", "tp", None),
        P("groups", "ctx", "tp", None),
        P("groups", "ctx", "tp", None),
        P(("groups", "ctx"), None, "tp", None),
        P(("groups", "ctx"), None, "tp", None),
        P("groups", None),
        P("tp", "ctx"),
    )
    return jax.shard_map(
        on_device, mesh=mesh, in_specs=placed, out_specs=P("groups", "tp", "ctx"), check_vma=False
    )
```

```python
import functools
import math

import jax
import jax.numpy as jnp
from jax import lax
from jax.experimental import pallas as pl
from jax.experimental.pallas import tpu as pltpu
from jax.sharding import PartitionSpec as P

NEGATIVE = -1e30
POSITIVE = 1e30
STATS = 3
OWN_ROWS = 16
GROUP = 8
LIMIT = 48 * 1024 * 1024

NT = (((1,), (1,)), ((), ()))
TN = (((0,), (0,)), ((), ()))


def whole(space=pltpu.VMEM):
    return pl.BlockSpec(memory_space=space)


def in_bf16(value):
    return value.astype(jnp.bfloat16).astype(jnp.float32)


def stat_rows(units):
    return -(-units * STATS // 16) * 16


class Sizes:
    def __init__(self, ranges, queries, cached, kv):
        self.n = ranges
        self.cand, self.toks, self.heads, self.width = queries
        self.kv = kv
        self.group = self.heads // kv
        self.blocks, self.block_tokens = cached[0], cached[1]
        self.lines = ranges // kv
        self.row_groups = self.lines // self.cand
        self.tokens = self.toks * ranges
        self.group_tokens = self.tokens // self.row_groups
        self.rows = self.group_tokens * self.group
        if kv != 4 or self.row_groups * self.cand * kv != ranges:
            raise ValueError("shape")


def place(size, line, first, second):
    me, core = lax.axis_index("ctx"), lax.axis_index("tp")
    other = (me // size.kv) ^ line
    return other * size.kv + ((me % size.kv) ^ (first * (1 + core)) ^ (second * (2 - core)))


def hop(size, value, stage):
    pairs = []
    cores = lax.axis_size("tp")
    for c in range(size.n):
        for core in range(cores):
            if stage == "first":
                other = c ^ (1 + core)
            elif stage == "second":
                other = c ^ (2 - core)
            else:
                other = c ^ (stage * size.kv)
            pairs.append((c * cores + core, other * cores + core))
    return lax.ppermute(value, ("ctx", "tp"), pairs)


def gather_lines(size, value):
    return jnp.stack([value] + [hop(size, value, k) for k in range(1, size.lines)])


def attention_kernel(size, second, firsts, lists, counts, qa, qb, keys, values, own_keys, own_values, *rest):
    outs, (rows, acc, tops, sums, stats) = rest[: len(firsts)], rest[len(firsts) :]
    units = 2 * size.lines
    half = size.rows // 2
    chip_rows = size.toks * size.group
    scale = size.width ** (-0.5) * math.log2(math.e)
    me, core = lax.axis_index("ctx"), lax.axis_index("tp")
    here, spot = me // size.kv, me % size.kv
    a_here = (spot >> core) & 1
    b_side = ((spot >> (1 - core)) & 1) ^ second
    for first, ref in enumerate((qa, qb)):
        for line in range(size.lines):
            other = here ^ line
            chip = (other % size.cand) * 2 + (a_here ^ first)
            for j in range(size.cand):
                parts = [ref[line, j, t].astype(jnp.float32) for t in range(size.toks)]
                for kv in range(size.kv):
                    cut = [p[kv * size.group : (kv + 1) * size.group] for p in parts]
                    rows[other // size.cand, j, kv, chip] = jnp.concatenate(cut).astype(jnp.bfloat16)
    heads = [place(size, 0, f, s) % size.kv for f in firsts for s in range(2)]

    def weighed(scores, live, before):
        high = before
        for s, alive in zip(scores, live):
            top = jnp.max(s, axis=0, keepdims=True) * scale
            top = in_bf16(top if alive is None else jnp.where(alive, top, NEGATIVE))
            high = top if high is None else jnp.maximum(high, top)
        weights, total = [], None
        for s, alive in zip(scores, live):
            shift = high if alive is None else jnp.where(alive, high, POSITIVE)
            p = jnp.exp2(s * scale - shift)
            part = jnp.sum(p, axis=0, keepdims=True)
            total = part if total is None else total + part
            weights.append(p.astype(jnp.bfloat16))
        return high, weights, total

    def blocks_of(j, head, q, g):
        slots = [g * GROUP + b for b in range(GROUP)]
        live = [slot < counts[j] for slot in slots]
        blocks = [lists[j, slot] for slot in slots]
        scores = [
            lax.dot_general(keys[head, block], q, NT, preferred_element_type=jnp.float32)
            for block in blocks
        ]
        return scores, live, [values[head, block] for block in blocks]

    def part(group, carry):
        lane = lax.broadcasted_iota(jnp.int32, (OWN_ROWS, half), 1)
        chip = lane // chip_rows
        line = group * size.cand + chip // 2
        chip = line * size.kv + ((chip % 2) << core) + (b_side << (1 - core))
        token = chip * size.toks + (lane % chip_rows) // size.group
        own = lax.broadcasted_iota(jnp.int32, (OWN_ROWS, half), 0)
        seen = (own < size.toks) & (own + me * size.toks <= token)
        for j in range(size.cand):
            for h, head in enumerate(heads):
                q = rows[group, j, head].reshape(half, size.width)
                s = lax.dot_general(
                    own_keys[j, head], q, NT, preferred_element_type=jnp.float32
                )
                scores, live, cut = blocks_of(j, head, q, 0)
                s = jnp.where(seen, s, NEGATIVE)
                scores, live, cut = [s] + scores, [None] + live, [own_values[j, head]] + cut
                high, weights, total = weighed(scores, live, None)
                none = high <= 0.5 * NEGATIVE * scale
                weights[0] = jnp.where(none, 0.0, weights[0].astype(jnp.float32)).astype(jnp.bfloat16)
                total = jnp.where(none, 0.0, total)
                acc[j, h] = lax.dot_general(
                    jnp.concatenate(cut), jnp.concatenate(weights), TN, preferred_element_type=jnp.float32
                )
                tops[j, h] = jnp.broadcast_to(high, (8, half))
                sums[j, h] = jnp.broadcast_to(total, (8, half))

        def more(j, carry):
            def over(g, carry):
                for h, head in enumerate(heads):
                    q = rows[group, j, head].reshape(half, size.width)
                    scores, live, cut = blocks_of(j, head, q, g)
                    before = tops[j, h, 0:1]
                    high, weights, total = weighed(scores, live, before)
                    fade = jnp.exp2(before - high)
                    acc[j, h] = acc[j, h] * fade + lax.dot_general(
                        jnp.concatenate(cut),
                        jnp.concatenate(weights),
                        TN,
                        preferred_element_type=jnp.float32,
                    )
                    sums[j, h] = jnp.broadcast_to(sums[j, h, 0:1] * fade + total, (8, half))
                    tops[j, h] = jnp.broadcast_to(high, (8, half))
                return carry

            return lax.fori_loop(1, (counts[j] + GROUP - 1) // GROUP, over, carry)

        lax.fori_loop(0, size.cand, more, 0)
        for j in range(size.cand):
            for h in range(len(heads)):
                out, unit = outs[h // 2], (h % 2) * size.lines + group * size.cand + j
                at = pl.multiple_of(unit * size.width, size.width)
                out[pl.ds(at, size.width), :] = acc[j, h].astype(jnp.bfloat16)
                l = sums[j, h, 0:1]
                rounded = in_bf16(l)
                stats[h // 2, pl.ds(unit, 1), :] = tops[j, h, 0:1]
                stats[h // 2, pl.ds(units + unit, 1), :] = rounded
                stats[h // 2, pl.ds(2 * units + unit, 1), :] = l - rounded
        return carry

    stats[...] = jnp.zeros_like(stats)
    lax.fori_loop(0, size.row_groups, part, 0)
    for f, out in enumerate(outs):
        out[pl.ds(units * size.width, stat_rows(units)), :] = stats[f].astype(jnp.bfloat16)


def attention_part(size, second, firsts, lists, counts, qa, qb, keys, values, own_keys, own_values):
    units, half = 2 * size.lines, size.rows // 2
    length = units * size.width + stat_rows(units)
    count = 2 * len(firsts)
    chips = size.n // size.row_groups // 2
    return pl.pallas_call(
        functools.partial(attention_kernel, size, second, firsts),
        out_shape=[jax.ShapeDtypeStruct((length, half), jnp.bfloat16)] * len(firsts),
        in_specs=[whole(pltpu.SMEM)] * 2 + [whole()] * 6,
        out_specs=[whole()] * len(firsts),
        scratch_shapes=[
            pltpu.VMEM(
                (size.row_groups, size.cand, size.kv, chips, size.toks * size.group, size.width),
                jnp.bfloat16,
            ),
            pltpu.VMEM((size.cand, count, size.width, half), jnp.float32),
            pltpu.VMEM((size.cand, count, 8, half), jnp.float32),
            pltpu.VMEM((size.cand, count, 8, half), jnp.float32),
            pltpu.VMEM((len(firsts), stat_rows(units), half), jnp.float32),
        ],
        compiler_params=pltpu.CompilerParams(vmem_limit_bytes=LIMIT),
        name="attention",
    )(lists, counts, qa, qb, keys, values, own_keys, own_values)


def merge_units(size, parts, firsts, stats_at, unit_lists, units_of):
    stats = []
    for ref, at, units, unit in zip(parts, stats_at, units_of, unit_lists):
        block = ref[pl.ds(at, stat_rows(units)), :].astype(jnp.float32)
        m = block[unit : unit + 1]
        l = block[units + unit : units + unit + 1] + block[2 * units + unit : 2 * units + unit + 1]
        stats.append((m, l))
    high = functools.reduce(jnp.maximum, [m for m, _ in stats])
    fades = [jnp.exp2(m - high) for m, _ in stats]
    total = functools.reduce(jnp.add, [l * f for (_, l), f in zip(stats, fades)])
    sums = None
    for ref, unit, fade in zip(parts, unit_lists, fades):
        value = ref[pl.ds(unit * size.width, size.width), :].astype(jnp.float32) * fade
        sums = value if sums is None else sums + value
    return sums, high, total


def merge_pair(size, mine, theirs, unit, units):
    at = units * size.width
    return merge_units(size, (mine, theirs), (0, 0), (at, at), (unit, unit), (units, units))


def merge_kernel(size, start, units, units_in, mine, theirs, out):
    highs, totals = [], []
    for unit in range(units):
        sums, high, total = merge_pair(size, mine, theirs, start + unit, units_in)
        out[pl.ds(unit * size.width, size.width), :] = sums.astype(jnp.bfloat16)
        highs.append(high)
        totals.append(total)
    lengths = [in_bf16(t) for t in totals]
    rows = highs + lengths + [t - l for t, l in zip(totals, lengths)]
    left = stat_rows(units) - len(rows)
    if left:
        rows.append(jnp.zeros((left, mine.shape[1]), jnp.float32))
    out[pl.ds(units * size.width, stat_rows(units)), :] = jnp.concatenate(rows).astype(jnp.bfloat16)


def merge(size, start, units, units_in, mine, theirs):
    length = units * size.width + stat_rows(units)
    return pl.pallas_call(
        functools.partial(merge_kernel, size, start, units, units_in),
        out_shape=jax.ShapeDtypeStruct((length, mine.shape[1]), jnp.bfloat16),
        in_specs=[whole()] * 2,
        out_specs=whole(),
        compiler_params=pltpu.CompilerParams(vmem_limit_bytes=LIMIT),
        name="merge",
    )(mine, theirs)


def split_kernel(size, near_mine, near_theirs, far_mine, far_theirs, *outs):
    here = lax.axis_index("ctx") // size.kv
    lines, width = size.lines, size.width
    for unit in range(lines):
        merged = [
            merge_pair(size, near_mine, near_theirs, unit, lines),
            merge_pair(size, far_mine, far_theirs, unit, lines),
        ]
        lengths = [in_bf16(total) for _, _, total in merged]
        tail = [high for _, high, _ in merged] + lengths
        tail += [total - length for (_, _, total), length in zip(merged, lengths)]
        tail.append(jnp.zeros((stat_rows(2) - len(tail), near_mine.shape[1]), jnp.float32))
        tail = jnp.concatenate(tail).astype(jnp.bfloat16)
        bodies = [sums.astype(jnp.bfloat16) for sums, _, _ in merged]
        for line, out in enumerate(outs):

            @pl.when((here ^ line) == unit)
            def _():
                out[:width, :] = bodies[0]
                out[width : 2 * width, :] = bodies[1]
                out[2 * width :, :] = tail


def split_merge(size, near_mine, near_theirs, far_mine, far_theirs):
    shape = jax.ShapeDtypeStruct((2 * size.width + stat_rows(2), size.rows // 2), jnp.bfloat16)
    return pl.pallas_call(
        functools.partial(split_kernel, size),
        out_shape=[shape] * size.lines,
        in_specs=[whole()] * 4,
        out_specs=[whole()] * size.lines,
        compiler_params=pltpu.CompilerParams(vmem_limit_bytes=LIMIT),
        name="split",
    )(near_mine, near_theirs, far_mine, far_theirs)


def finish_kernel(size, *refs):
    parts, out, turned = refs[:-2], refs[-2], refs[-1]
    count = len(parts)
    chip_rows = size.toks * size.group
    spot, core = lax.axis_index("ctx") % size.kv, lax.axis_index("tp")
    b_here = (spot >> (1 - core)) & 1
    for side in range(2):
        at = 2 * size.width
        sums, _, total = merge_units(
            size, parts, (0,) * count, (at,) * count, (side,) * count, (2,) * count
        )
        half = (sums / total).T
        for chip in range(size.n // size.row_groups // 2):
            absolute = chip // 2 * size.kv + ((chip % 2) << core) + ((b_here ^ side) << (1 - core))
            to = pl.multiple_of(absolute * chip_rows, chip_rows)
            turned[pl.ds(to, chip_rows), :] = half[chip * chip_rows : (chip + 1) * chip_rows]
    for g in range(size.group):
        piece = turned[pl.ds(g, size.group_tokens, stride=size.group), :]
        out[pl.ds(g * size.group_tokens, size.group_tokens), :] = piece.astype(jnp.bfloat16)


def finish(size, parts):
    return pl.pallas_call(
        functools.partial(finish_kernel, size),
        out_shape=jax.ShapeDtypeStruct((size.rows, size.width), jnp.bfloat16),
        in_specs=[whole()] * len(parts),
        out_specs=whole(),
        scratch_shapes=[pltpu.VMEM((size.rows, size.width), jnp.float32)],
        compiler_params=pltpu.CompilerParams(vmem_limit_bytes=LIMIT),
        name="finish",
    )(*parts)


def project_kernel(size, a0, a1, a2, a3, weight, kept, sent, whole_rows, product):
    core = lax.axis_index("tp")
    for index, ref in enumerate((a0, a1, a2, a3)):
        for line in range(size.lines):
            chip = place(size, line, index % 2, index // 2)
            kv, other = chip % size.kv, chip // size.kv
            j, part = other % size.cand, other // size.cand
            at = pl.multiple_of(j * size.tokens + part * size.group_tokens, size.group_tokens)
            for g in range(size.group):
                piece = ref[line, pl.ds(g * size.group_tokens, size.group_tokens), :]
                whole_rows[kv * size.group + g, pl.ds(at, size.group_tokens), :] = piece
    total = None
    for h in range(0, size.heads, 2):
        pair = jnp.concatenate([whole_rows[h], whole_rows[h + 1]], axis=1)
        term = jnp.dot(
            pair,
            weight[pl.ds(h * size.width, 2 * size.width), :],
            preferred_element_type=jnp.float32,
        )
        total = term if total is None else total + term
    product[...] = total
    half = size.tokens // 2
    for j in range(size.cand):
        near = pl.multiple_of(j * size.tokens + core * half, half)
        far = pl.multiple_of(j * size.tokens + (1 - core) * half, half)
        kept[j] = product[pl.ds(near, half), :]
        sent[j] = product[pl.ds(far, half), :].astype(jnp.bfloat16)


def project(size, gathered, weight):
    columns = weight.shape[1]
    shape = (size.cand, size.tokens // 2, columns)
    return pl.pallas_call(
        functools.partial(project_kernel, size),
        out_shape=[
            jax.ShapeDtypeStruct(shape, jnp.float32),
            jax.ShapeDtypeStruct(shape, jnp.bfloat16),
        ],
        in_specs=[whole()] * 5,
        out_specs=[whole()] * 2,
        scratch_shapes=[
            pltpu.VMEM((size.heads, size.cand * size.tokens, size.width), jnp.bfloat16),
            pltpu.VMEM((size.cand * size.tokens, columns), jnp.float32),
        ],
        compiler_params=pltpu.CompilerParams(vmem_limit_bytes=LIMIT),
        name="project",
    )(*gathered, weight)


def gather_all(size, value):
    a0 = gather_lines(size, value)
    a1 = hop(size, a0, "first")
    a2 = hop(size, a0, "second")
    a3 = hop(size, a1, "second")
    return a0, a1, a2, a3


def listed_here(size, block_lists):
    lowest = lax.axis_index("ctx") * size.blocks
    local = block_lists - lowest
    below = jnp.sum((local < 0).astype(jnp.int32), axis=1)
    inside = jnp.sum((local < size.blocks).astype(jnp.int32), axis=1) - below
    slots = jnp.arange(-(-size.blocks // GROUP) * GROUP)
    entry = jnp.arange(block_lists.shape[1])
    hit = entry[None, None, :] == (below[:, None] + slots[None, :])[:, :, None]
    hit = hit & (slots[None, :] < inside[:, None])[:, :, None]
    return jnp.sum(jnp.where(hit, local[:, None, :], 0), axis=2), inside


def on_device(
    queries,
    cand_keys,
    candidate_values,
    cached_prompt_keys,
    cached_prompt_values,
    block_lists,
    out_weight,
):
    size = Sizes(
        lax.axis_size("ctx"), queries.shape, cached_prompt_keys.shape, cand_keys.shape[2]
    )
    lists, counts = listed_here(size, block_lists)
    keys = jnp.transpose(cached_prompt_keys, (2, 0, 1, 3))
    values = jnp.transpose(cached_prompt_values, (2, 0, 1, 3))
    room = ((0, 0), (0, 0), (0, OWN_ROWS - size.toks), (0, 0))
    own_keys = jnp.pad(jnp.transpose(cand_keys, (0, 2, 1, 3)), room)
    own_values = jnp.pad(jnp.transpose(candidate_values, (0, 2, 1, 3)), room)
    moved = [queries] + [hop(size, queries, k) for k in range(1, size.lines)]
    ready = (lists, counts, keys, values, own_keys, own_values)
    moved, ready = lax.optimization_barrier((moved, ready))
    lists, counts, keys, values, own_keys, own_values = ready
    q0 = jnp.stack(moved)
    q1, q2 = hop(size, q0, "first"), hop(size, q0, "second")
    q3 = hop(size, q1, "second")
    lines, units = size.lines, 2 * size.lines
    near_away, near = attention_part(size, 0, (1, 0), lists, counts, q0, q1, *ready[2:])
    near_away = hop(size, near_away, "first")
    (far_away,) = attention_part(size, 1, (1,), lists, counts, q2, q3, *ready[2:])
    far_away = hop(size, far_away, "first")
    (far,) = attention_part(size, 1, (0,), lists, counts, q2, q3, *ready[2:])
    near_leaves = hop(size, merge(size, lines, lines, units, near, near_away), "second")
    near_stays = merge(size, 0, lines, units, near, near_away)
    far_leaves = hop(size, merge(size, lines, lines, units, far, far_away), "second")
    far_stays = merge(size, 0, lines, units, far, far_away)
    parts = split_merge(size, near_stays, far_leaves, far_stays, near_leaves)
    parts = [parts[0]] + [hop(size, parts[k], k) for k in range(1, lines)]
    attention = finish(size, parts)
    kept, sent = project(size, gather_all(size, attention), out_weight)
    cores = lax.axis_size("tp")
    sent = lax.ppermute(sent, "tp", [(i, cores - 1 - i) for i in range(cores)])
    return (kept + sent.astype(jnp.float32)).astype(jnp.bfloat16)


def solution(mesh):
    placed = (
        P("groups", "ctx", "tp", None),
        P("groups", "ctx", "tp", None),
        P("groups", "ctx", "tp", None),
        P(("groups", "ctx"), None, "tp", None),
        P(("groups", "ctx"), None, "tp", None),
        P("groups", None),
        P("tp", "ctx"),
    )
    return jax.shard_map(
        on_device, mesh=mesh, in_specs=placed, out_specs=P("groups", "tp", "ctx"), check_vma=False
    )
```

```python
import functools
import math

import jax
import jax.numpy as jnp
from jax import lax
from jax.experimental import pallas as pl
from jax.experimental.pallas import tpu as pltpu
from jax.sharding import PartitionSpec as P

NEGATIVE = -1e30
POSITIVE = 1e30
STATS = 3
OWN_ROWS = 16
GROUP = 8
LIMIT = 48 * 1024 * 1024

NT = (((1,), (1,)), ((), ()))
TN = (((0,), (0,)), ((), ()))


def whole(space=pltpu.VMEM):
    return pl.BlockSpec(memory_space=space)


def in_bf16(value):
    return value.astype(jnp.bfloat16).astype(jnp.float32)


def stat_rows(units):
    return -(-units * STATS // 16) * 16


class Sizes:
    def __init__(self, ranges, queries, cached, kv):
        self.n = ranges
        self.cand, self.toks, self.heads, self.width = queries
        self.kv = kv
        self.group = self.heads // kv
        self.blocks, self.block_tokens = cached[0], cached[1]
        self.lines = ranges // kv
        self.row_groups = self.lines // self.cand
        self.tokens = self.toks * ranges
        self.group_tokens = self.tokens // self.row_groups
        self.rows = self.group_tokens * self.group
        if kv != 4 or self.row_groups * self.cand * kv != ranges:
            raise ValueError("shape")


def place(size, line, first, second):
    me, core = lax.axis_index("ctx"), lax.axis_index("tp")
    other = (me // size.kv) ^ line
    return other * size.kv + ((me % size.kv) ^ (first * (1 + core)) ^ (second * (2 - core)))


def hop(size, value, stage):
    pairs = []
    cores = lax.axis_size("tp")
    for c in range(size.n):
        for core in range(cores):
            if stage == "first":
                other = c ^ (1 + core)
            elif stage == "second":
                other = c ^ (2 - core)
            else:
                other = c ^ (stage * size.kv)
            pairs.append((c * cores + core, other * cores + core))
    return lax.ppermute(value, ("ctx", "tp"), pairs)


def gather_lines(size, value):
    return jnp.stack([value] + [hop(size, value, k) for k in range(1, size.lines)])


def attention_kernel(size, second, firsts, lists, counts, qa, qb, keys, values, own_keys, own_values, *rest):
    outs, (rows, acc, first_scores, tops, sums, stats) = rest[: len(firsts)], rest[len(firsts) :]
    units = 2 * size.lines
    half = size.rows // 2
    chip_rows = size.toks * size.group
    scale = size.width ** (-0.5) * math.log2(math.e)
    me, core = lax.axis_index("ctx"), lax.axis_index("tp")
    here, spot = me // size.kv, me % size.kv
    a_here = (spot >> core) & 1
    b_side = ((spot >> (1 - core)) & 1) ^ second
    for first, ref in enumerate((qa, qb)):
        for line in range(size.lines):
            other = here ^ line
            chip = (other % size.cand) * 2 + (a_here ^ first)
            for j in range(size.cand):
                parts = [ref[line, j, t].astype(jnp.float32) for t in range(size.toks)]
                for kv in range(size.kv):
                    cut = [p[kv * size.group : (kv + 1) * size.group] for p in parts]
                    rows[other // size.cand, j, kv, chip] = jnp.concatenate(cut).astype(jnp.bfloat16)
    heads = [place(size, 0, f, s) % size.kv for f in firsts for s in range(2)]

    def weighed(scores, live, before, own_top):
        highs = [
            jnp.where(alive, jnp.max(s.reshape(-1, 8, half), axis=0) * scale, NEGATIVE)
            for s, alive in zip(scores, live)
        ]
        if own_top is not None:
            highs.append(own_top)
        high = in_bf16(jnp.max(functools.reduce(jnp.maximum, highs), axis=0, keepdims=True))
        fade = None
        if before is not None:
            high = jnp.maximum(before, high)
            fade = jnp.exp2(before - high)
        weights, total = [], None
        for s, alive in zip(scores, live):
            p = jnp.exp2(s * scale - jnp.where(alive, high, POSITIVE))
            part = jnp.sum(p.reshape(-1, 8, half), axis=0)
            total = part if total is None else total + part
            weights.append(p.astype(jnp.bfloat16))
        return high, weights, total, fade

    def blocks_of(j, head, q, g):
        slots = [g * GROUP + b for b in range(GROUP)]
        live = [slot < counts[j] for slot in slots]
        blocks = [lists[j, slot] for slot in slots]
        scores = lax.dot_general(
            jnp.concatenate([keys[head, block] for block in blocks]),
            q,
            NT,
            preferred_element_type=jnp.float32,
        )
        scores = [scores[b * size.block_tokens : (b + 1) * size.block_tokens] for b in range(GROUP)]
        return scores, live, [values[head, block] for block in blocks]

    def gathered_values(cut, weights):
        return lax.dot_general(
            jnp.concatenate(cut), jnp.concatenate(weights), TN, preferred_element_type=jnp.float32
        )

    def part(group, carry):
        lane = lax.broadcasted_iota(jnp.int32, (OWN_ROWS, half), 1)
        chip = lane // chip_rows
        line = group * size.cand + chip // 2
        chip = line * size.kv + ((chip % 2) << core) + (b_side << (1 - core))
        token = chip * size.toks + (lane % chip_rows) // size.group
        own = lax.broadcasted_iota(jnp.int32, (OWN_ROWS, half), 0)
        seen = (own < size.toks) & (own + me * size.toks <= token)
        for j in range(size.cand):
            for h, head in enumerate(heads):
                q = rows[group, j, head].reshape(half, size.width)
                s = lax.dot_general(own_keys[j, head], q, NT, preferred_element_type=jnp.float32)
                first_scores[j, h] = jnp.where(seen, s * scale, NEGATIVE)

        work = [(j, h) for j in range(size.cand) for h in range(len(heads))]
        found = []
        for j, h in work:
            q = rows[group, j, heads[h]].reshape(half, size.width)
            found.append(blocks_of(j, heads[h], q, 0))
        for (j, h), (scores, live, cut) in zip(work, found):
            own_scores = first_scores[j, h]
            own_top = jnp.max(own_scores.reshape(-1, 8, half), axis=0)
            high, weights, total, _ = weighed(scores, live, None, own_top)
            p = jnp.where(seen, jnp.exp2(own_scores - high), 0.0)
            total = total + jnp.sum(p.reshape(-1, 8, half), axis=0)
            acc[j, h] = gathered_values(
                cut + [own_values[j, heads[h]]], weights + [p.astype(jnp.bfloat16)]
            )
            tops[j, h] = jnp.broadcast_to(high, (8, half))
            sums[j, h] = total

        def more(j, carry):
            def over(g, carry):
                found = []
                for head in heads:
                    q = rows[group, j, head].reshape(half, size.width)
                    found.append(blocks_of(j, head, q, g))
                for h, (scores, live, cut) in enumerate(found):
                    before = tops[j, h, 0:1]
                    high, weights, total, fade = weighed(scores, live, before, None)
                    acc[j, h] = acc[j, h] * fade + gathered_values(cut, weights)
                    sums[j, h] = sums[j, h] * fade + total
                    tops[j, h] = jnp.broadcast_to(high, (8, half))
                return carry

            return lax.fori_loop(1, (counts[j] + GROUP - 1) // GROUP, over, carry)

        lax.fori_loop(0, size.cand, more, 0)
        for j in range(size.cand):
            for h in range(len(heads)):
                out, unit = outs[h // 2], (h % 2) * size.lines + group * size.cand + j
                at = pl.multiple_of(unit * size.width, size.width)
                out[pl.ds(at, size.width), :] = acc[j, h].astype(jnp.bfloat16)
                l = jnp.sum(sums[j, h], axis=0, keepdims=True)
                rounded = in_bf16(l)
                stats[h // 2, pl.ds(unit, 1), :] = tops[j, h, 0:1]
                stats[h // 2, pl.ds(units + unit, 1), :] = rounded
                stats[h // 2, pl.ds(2 * units + unit, 1), :] = l - rounded
        return carry

    stats[...] = jnp.zeros_like(stats)
    lax.fori_loop(0, size.row_groups, part, 0)
    for f, out in enumerate(outs):
        out[pl.ds(units * size.width, stat_rows(units)), :] = stats[f].astype(jnp.bfloat16)


def attention_part(size, second, firsts, lists, counts, qa, qb, keys, values, own_keys, own_values):
    units, half = 2 * size.lines, size.rows // 2
    length = units * size.width + stat_rows(units)
    count = 2 * len(firsts)
    chips = size.n // size.row_groups // 2
    return pl.pallas_call(
        functools.partial(attention_kernel, size, second, firsts),
        out_shape=[jax.ShapeDtypeStruct((length, half), jnp.bfloat16)] * len(firsts),
        in_specs=[whole(pltpu.SMEM)] * 2 + [whole()] * 6,
        out_specs=[whole()] * len(firsts),
        scratch_shapes=[
            pltpu.VMEM(
                (size.row_groups, size.cand, size.kv, chips, size.toks * size.group, size.width),
                jnp.bfloat16,
            ),
            pltpu.VMEM((size.cand, count, size.width, half), jnp.float32),
            pltpu.VMEM((size.cand, count, OWN_ROWS, half), jnp.float32),
            pltpu.VMEM((size.cand, count, 8, half), jnp.float32),
            pltpu.VMEM((size.cand, count, 8, half), jnp.float32),
            pltpu.VMEM((len(firsts), stat_rows(units), half), jnp.float32),
        ],
        compiler_params=pltpu.CompilerParams(vmem_limit_bytes=LIMIT),
        name="attention",
    )(lists, counts, qa, qb, keys, values, own_keys, own_values)


def merge_units(size, parts, firsts, stats_at, unit_lists, units_of):
    stats = []
    for ref, at, units, unit in zip(parts, stats_at, units_of, unit_lists):
        block = ref[pl.ds(at, stat_rows(units)), :].astype(jnp.float32)
        m = block[unit : unit + 1]
        l = block[units + unit : units + unit + 1] + block[2 * units + unit : 2 * units + unit + 1]
        stats.append((m, l))
    high = functools.reduce(jnp.maximum, [m for m, _ in stats])
    fades = [jnp.exp2(m - high) for m, _ in stats]
    total = functools.reduce(jnp.add, [l * f for (_, l), f in zip(stats, fades)])
    sums = None
    for ref, unit, fade in zip(parts, unit_lists, fades):
        value = ref[pl.ds(unit * size.width, size.width), :].astype(jnp.float32) * fade
        sums = value if sums is None else sums + value
    return sums, high, total


def merge_pair(size, mine, theirs, unit, units):
    at = units * size.width
    return merge_units(size, (mine, theirs), (0, 0), (at, at), (unit, unit), (units, units))


def merge_kernel(size, start, units, units_in, mine, theirs, out):
    highs, totals = [], []
    for unit in range(units):
        sums, high, total = merge_pair(size, mine, theirs, start + unit, units_in)
        out[pl.ds(unit * size.width, size.width), :] = sums.astype(jnp.bfloat16)
        highs.append(high)
        totals.append(total)
    lengths = [in_bf16(t) for t in totals]
    rows = highs + lengths + [t - l for t, l in zip(totals, lengths)]
    left = stat_rows(units) - len(rows)
    if left:
        rows.append(jnp.zeros((left, mine.shape[1]), jnp.float32))
    out[pl.ds(units * size.width, stat_rows(units)), :] = jnp.concatenate(rows).astype(jnp.bfloat16)


def merge(size, start, units, units_in, mine, theirs):
    length = units * size.width + stat_rows(units)
    return pl.pallas_call(
        functools.partial(merge_kernel, size, start, units, units_in),
        out_shape=jax.ShapeDtypeStruct((length, mine.shape[1]), jnp.bfloat16),
        in_specs=[whole()] * 2,
        out_specs=whole(),
        compiler_params=pltpu.CompilerParams(vmem_limit_bytes=LIMIT),
        name="merge",
    )(mine, theirs)


def split_kernel(size, near_mine, near_theirs, far_mine, far_theirs, *outs):
    here = lax.axis_index("ctx") // size.kv
    lines, width = size.lines, size.width
    for unit in range(lines):
        merged = [
            merge_pair(size, near_mine, near_theirs, unit, lines),
            merge_pair(size, far_mine, far_theirs, unit, lines),
        ]
        lengths = [in_bf16(total) for _, _, total in merged]
        tail = [high for _, high, _ in merged] + lengths
        tail += [total - length for (_, _, total), length in zip(merged, lengths)]
        tail.append(jnp.zeros((stat_rows(2) - len(tail), near_mine.shape[1]), jnp.float32))
        tail = jnp.concatenate(tail).astype(jnp.bfloat16)
        bodies = [sums.astype(jnp.bfloat16) for sums, _, _ in merged]
        for line, out in enumerate(outs):

            @pl.when((here ^ line) == unit)
            def _():
                out[:width, :] = bodies[0]
                out[width : 2 * width, :] = bodies[1]
                out[2 * width :, :] = tail


def split_merge(size, near_mine, near_theirs, far_mine, far_theirs):
    shape = jax.ShapeDtypeStruct((2 * size.width + stat_rows(2), size.rows // 2), jnp.bfloat16)
    return pl.pallas_call(
        functools.partial(split_kernel, size),
        out_shape=[shape] * size.lines,
        in_specs=[whole()] * 4,
        out_specs=[whole()] * size.lines,
        compiler_params=pltpu.CompilerParams(vmem_limit_bytes=LIMIT),
        name="split",
    )(near_mine, near_theirs, far_mine, far_theirs)


def finish_kernel(size, *refs):
    parts, out, turned = refs[:-2], refs[-2], refs[-1]
    count = len(parts)
    chip_rows = size.toks * size.group
    spot, core = lax.axis_index("ctx") % size.kv, lax.axis_index("tp")
    b_here = (spot >> (1 - core)) & 1
    for side in range(2):
        at = 2 * size.width
        sums, _, total = merge_units(
            size, parts, (0,) * count, (at,) * count, (side,) * count, (2,) * count
        )
        half = (sums / total).T
        for chip in range(size.n // size.row_groups // 2):
            absolute = chip // 2 * size.kv + ((chip % 2) << core) + ((b_here ^ side) << (1 - core))
            to = pl.multiple_of(absolute * chip_rows, chip_rows)
            turned[pl.ds(to, chip_rows), :] = half[chip * chip_rows : (chip + 1) * chip_rows]
    for g in range(size.group):
        piece = turned[pl.ds(g, size.group_tokens, stride=size.group), :]
        out[pl.ds(g * size.group_tokens, size.group_tokens), :] = piece.astype(jnp.bfloat16)


def finish(size, parts):
    return pl.pallas_call(
        functools.partial(finish_kernel, size),
        out_shape=jax.ShapeDtypeStruct((size.rows, size.width), jnp.bfloat16),
        in_specs=[whole()] * len(parts),
        out_specs=whole(),
        scratch_shapes=[pltpu.VMEM((size.rows, size.width), jnp.float32)],
        compiler_params=pltpu.CompilerParams(vmem_limit_bytes=LIMIT),
        name="finish",
    )(*parts)


def project_kernel(size, a0, a1, a2, a3, weight, kept, sent, whole_rows, product):
    core = lax.axis_index("tp")
    for index, ref in enumerate((a0, a1, a2, a3)):
        for line in range(size.lines):
            chip = place(size, line, index % 2, index // 2)
            kv, other = chip % size.kv, chip // size.kv
            j, part = other % size.cand, other // size.cand
            at = pl.multiple_of(j * size.tokens + part * size.group_tokens, size.group_tokens)
            for g in range(size.group):
                piece = ref[line, pl.ds(g * size.group_tokens, size.group_tokens), :]
                whole_rows[kv * size.group + g, pl.ds(at, size.group_tokens), :] = piece
    total = None
    for h in range(0, size.heads, 2):
        pair = jnp.concatenate([whole_rows[h], whole_rows[h + 1]], axis=1)
        term = jnp.dot(
            pair,
            weight[pl.ds(h * size.width, 2 * size.width), :],
            preferred_element_type=jnp.float32,
        )
        total = term if total is None else total + term
    product[...] = total
    half = size.tokens // 2
    for j in range(size.cand):
        near = pl.multiple_of(j * size.tokens + core * half, half)
        far = pl.multiple_of(j * size.tokens + (1 - core) * half, half)
        kept[j] = product[pl.ds(near, half), :]
        sent[j] = product[pl.ds(far, half), :].astype(jnp.bfloat16)


def project(size, gathered, weight):
    columns = weight.shape[1]
    shape = (size.cand, size.tokens // 2, columns)
    return pl.pallas_call(
        functools.partial(project_kernel, size),
        out_shape=[
            jax.ShapeDtypeStruct(shape, jnp.float32),
            jax.ShapeDtypeStruct(shape, jnp.bfloat16),
        ],
        in_specs=[whole()] * 5,
        out_specs=[whole()] * 2,
        scratch_shapes=[
            pltpu.VMEM((size.heads, size.cand * size.tokens, size.width), jnp.bfloat16),
            pltpu.VMEM((size.cand * size.tokens, columns), jnp.float32),
        ],
        compiler_params=pltpu.CompilerParams(vmem_limit_bytes=LIMIT),
        name="project",
    )(*gathered, weight)


def gather_all(size, value):
    a0 = gather_lines(size, value)
    a1 = hop(size, a0, "first")
    a2 = hop(size, a0, "second")
    a3 = hop(size, a1, "second")
    return a0, a1, a2, a3


def listed_here(size, block_lists):
    lowest = lax.axis_index("ctx") * size.blocks
    local = block_lists - lowest
    below = jnp.sum((local < 0).astype(jnp.int32), axis=1)
    inside = jnp.sum((local < size.blocks).astype(jnp.int32), axis=1) - below
    slots = jnp.arange(-(-size.blocks // GROUP) * GROUP)
    entry = jnp.arange(block_lists.shape[1])
    hit = entry[None, None, :] == (below[:, None] + slots[None, :])[:, :, None]
    hit = hit & (slots[None, :] < inside[:, None])[:, :, None]
    return jnp.sum(jnp.where(hit, local[:, None, :], 0), axis=2), inside


def on_device(
    queries,
    cand_keys,
    candidate_values,
    cached_prompt_keys,
    cached_prompt_values,
    block_lists,
    out_weight,
):
    size = Sizes(
        lax.axis_size("ctx"), queries.shape, cached_prompt_keys.shape, cand_keys.shape[2]
    )
    lists, counts = listed_here(size, block_lists)
    keys = jnp.transpose(cached_prompt_keys, (2, 0, 1, 3))
    values = jnp.transpose(cached_prompt_values, (2, 0, 1, 3))
    room = ((0, 0), (0, 0), (0, OWN_ROWS - size.toks), (0, 0))
    own_keys = jnp.pad(jnp.transpose(cand_keys, (0, 2, 1, 3)), room)
    own_values = jnp.pad(jnp.transpose(candidate_values, (0, 2, 1, 3)), room)
    moved = [queries] + [hop(size, queries, k) for k in range(1, size.lines)]
    ready = (lists, counts, keys, values, own_keys, own_values)
    moved, ready = lax.optimization_barrier((moved, ready))
    lists, counts, keys, values, own_keys, own_values = ready
    q0 = jnp.stack(moved)
    q1, q2 = hop(size, q0, "first"), hop(size, q0, "second")
    q3 = hop(size, q1, "second")
    lines, units = size.lines, 2 * size.lines
    near_away, near = attention_part(size, 0, (1, 0), lists, counts, q0, q1, *ready[2:])
    near_away = hop(size, near_away, "first")
    (far_away,) = attention_part(size, 1, (1,), lists, counts, q2, q3, *ready[2:])
    far_away = hop(size, far_away, "first")
    (far,) = attention_part(size, 1, (0,), lists, counts, q2, q3, *ready[2:])
    near_leaves = hop(size, merge(size, lines, lines, units, near, near_away), "second")
    near_stays = merge(size, 0, lines, units, near, near_away)
    far_leaves = hop(size, merge(size, lines, lines, units, far, far_away), "second")
    far_stays = merge(size, 0, lines, units, far, far_away)
    parts = split_merge(size, near_stays, far_leaves, far_stays, near_leaves)
    parts = [parts[0]] + [hop(size, parts[k], k) for k in range(1, lines)]
    attention = finish(size, parts)
    kept, sent = project(size, gather_all(size, attention), out_weight)
    cores = lax.axis_size("tp")
    sent = lax.ppermute(sent, "tp", [(i, cores - 1 - i) for i in range(cores)])
    return (kept + sent.astype(jnp.float32)).astype(jnp.bfloat16)


def solution(mesh):
    placed = (
        P("groups", "ctx", "tp", None),
        P("groups", "ctx", "tp", None),
        P("groups", "ctx", "tp", None),
        P(("groups", "ctx"), None, "tp", None),
        P(("groups", "ctx"), None, "tp", None),
        P("groups", None),
        P("tp", "ctx"),
    )
    return jax.shard_map(
        on_device, mesh=mesh, in_specs=placed, out_specs=P("groups", "tp", "ctx"), check_vma=False
    )
```

```python
import functools
import math

import jax
import jax.numpy as jnp
from jax import lax
from jax.experimental import pallas as pl
from jax.experimental.pallas import tpu as pltpu
from jax.sharding import PartitionSpec as P

NEGATIVE = -1e30
POSITIVE = 1e30
STATS = 3
OWN_ROWS = 16
GROUP = 8
LIMIT = 48 * 1024 * 1024

NT = (((1,), (1,)), ((), ()))
TN = (((0,), (0,)), ((), ()))


def whole(space=pltpu.VMEM):
    return pl.BlockSpec(memory_space=space)


def in_bf16(value):
    return value.astype(jnp.bfloat16).astype(jnp.float32)


def stat_rows(units):
    return -(-units * STATS // 16) * 16


class Sizes:
    def __init__(self, ranges, queries, cached, kv):
        self.n = ranges
        self.cand, self.toks, self.heads, self.width = queries
        self.kv = kv
        self.group = self.heads // kv
        self.blocks, self.block_tokens = cached[0], cached[1]
        self.lines = ranges // kv
        self.row_groups = self.lines // self.cand
        self.tokens = self.toks * ranges
        self.group_tokens = self.tokens // self.row_groups
        self.rows = self.group_tokens * self.group
        if kv != 4 or self.row_groups * self.cand * kv != ranges:
            raise ValueError("shape")


def place(size, line, first, second):
    me, core = lax.axis_index("ctx"), lax.axis_index("tp")
    other = (me // size.kv) ^ line
    return other * size.kv + ((me % size.kv) ^ (first * (1 + core)) ^ (second * (2 - core)))


def hop(size, value, stage):
    pairs = []
    cores = lax.axis_size("tp")
    for c in range(size.n):
        for core in range(cores):
            if stage == "first":
                other = c ^ (1 + core)
            elif stage == "second":
                other = c ^ (2 - core)
            elif stage == "both":
                other = c ^ 3
            else:
                other = c ^ (stage * size.kv)
            pairs.append((c * cores + core, other * cores + core))
    return lax.ppermute(value, ("ctx", "tp"), pairs)


def gather_lines(size, value):
    return jnp.stack([value] + [hop(size, value, k) for k in range(1, size.lines)])


def attention_kernel(size, far, places, lists, counts, qa, qb, keys, values, own_keys, own_values, *rest):
    outs, (rows, acc, first_scores, tops, sums, stats) = rest[: len(places)], rest[len(places) :]
    units = size.lines
    half = size.rows // 2
    chip_rows = size.toks * size.group
    scale = size.width ** (-0.5) * math.log2(math.e)
    me, core = lax.axis_index("ctx"), lax.axis_index("tp")
    here, spot = me // size.kv, me % size.kv
    a_here = (spot >> core) & 1
    b_side = ((spot >> (1 - core)) & 1) ^ far
    for first, ref in enumerate((qa, qb)):
        for line in range(size.lines):
            other = here ^ line
            chip = (other % size.cand) * 2 + (a_here ^ first)
            for j in range(size.cand):
                parts = [ref[line, j, t].astype(jnp.float32) for t in range(size.toks)]
                for kv in range(size.kv):
                    cut = [p[kv * size.group : (kv + 1) * size.group] for p in parts]
                    rows[other // size.cand, j, kv, chip] = jnp.concatenate(cut).astype(jnp.bfloat16)
    heads = [place(size, 0, *at) % size.kv for at in places]

    def weighed(scores, live, before, own_top):
        highs = [
            jnp.where(alive, jnp.max(s.reshape(-1, 8, half), axis=0) * scale, NEGATIVE)
            for s, alive in zip(scores, live)
        ]
        if own_top is not None:
            highs.append(own_top)
        high = in_bf16(jnp.max(functools.reduce(jnp.maximum, highs), axis=0, keepdims=True))
        fade = None
        if before is not None:
            high = jnp.maximum(before, high)
            fade = jnp.exp2(before - high)
        weights, total = [], None
        for s, alive in zip(scores, live):
            p = jnp.exp2(s * scale - jnp.where(alive, high, POSITIVE))
            part = jnp.sum(p.reshape(-1, 8, half), axis=0)
            total = part if total is None else total + part
            weights.append(p.astype(jnp.bfloat16))
        return high, weights, total, fade

    def blocks_of(j, head, q, g):
        slots = [g * GROUP + b for b in range(GROUP)]
        live = [slot < counts[j] for slot in slots]
        blocks = [lists[j, slot] for slot in slots]
        scores = lax.dot_general(
            jnp.concatenate([keys[head, block] for block in blocks]),
            q,
            NT,
            preferred_element_type=jnp.float32,
        )
        scores = [scores[b * size.block_tokens : (b + 1) * size.block_tokens] for b in range(GROUP)]
        return scores, live, [values[head, block] for block in blocks]

    def gathered_values(cut, weights):
        return lax.dot_general(
            jnp.concatenate(cut), jnp.concatenate(weights), TN, preferred_element_type=jnp.float32
        )

    def part(group, carry):
        lane = lax.broadcasted_iota(jnp.int32, (OWN_ROWS, half), 1)
        chip = lane // chip_rows
        line = group * size.cand + chip // 2
        chip = line * size.kv + ((chip % 2) << core) + (b_side << (1 - core))
        token = chip * size.toks + (lane % chip_rows) // size.group
        own = lax.broadcasted_iota(jnp.int32, (OWN_ROWS, half), 0)
        seen = (own < size.toks) & (own + me * size.toks <= token)
        for j in range(size.cand):
            for h, head in enumerate(heads):
                q = rows[group, j, head].reshape(half, size.width)
                s = lax.dot_general(own_keys[j, head], q, NT, preferred_element_type=jnp.float32)
                first_scores[j, h] = jnp.where(seen, s * scale, NEGATIVE)

        work = [(j, h) for j in range(size.cand) for h in range(len(heads))]
        found = []
        for j, h in work:
            q = rows[group, j, heads[h]].reshape(half, size.width)
            found.append(blocks_of(j, heads[h], q, 0))
        for (j, h), (scores, live, cut) in zip(work, found):
            own_scores = first_scores[j, h]
            own_top = jnp.max(own_scores.reshape(-1, 8, half), axis=0)
            high, weights, total, _ = weighed(scores, live, None, own_top)
            p = jnp.where(seen, jnp.exp2(own_scores - high), 0.0)
            total = total + jnp.sum(p.reshape(-1, 8, half), axis=0)
            acc[j, h] = gathered_values(
                cut + [own_values[j, heads[h]]], weights + [p.astype(jnp.bfloat16)]
            )
            tops[j, h] = jnp.broadcast_to(high, (8, half))
            sums[j, h] = total

        def more(j, carry):
            def over(g, carry):
                found = []
                for head in heads:
                    q = rows[group, j, head].reshape(half, size.width)
                    found.append(blocks_of(j, head, q, g))
                for h, (scores, live, cut) in enumerate(found):
                    before = tops[j, h, 0:1]
                    high, weights, total, fade = weighed(scores, live, before, None)
                    acc[j, h] = acc[j, h] * fade + gathered_values(cut, weights)
                    sums[j, h] = sums[j, h] * fade + total
                    tops[j, h] = jnp.broadcast_to(high, (8, half))
                return carry

            return lax.fori_loop(1, (counts[j] + GROUP - 1) // GROUP, over, carry)

        lax.fori_loop(0, size.cand, more, 0)
        for j in range(size.cand):
            for h in range(len(heads)):
                out, unit = outs[h], group * size.cand + j
                at = pl.multiple_of(unit * size.width, size.width)
                out[pl.ds(at, size.width), :] = acc[j, h].astype(jnp.bfloat16)
                l = jnp.sum(sums[j, h], axis=0, keepdims=True)
                rounded = in_bf16(l)
                stats[h, pl.ds(unit, 1), :] = tops[j, h, 0:1]
                stats[h, pl.ds(units + unit, 1), :] = rounded
                stats[h, pl.ds(2 * units + unit, 1), :] = l - rounded
        return carry

    stats[...] = jnp.zeros_like(stats)
    lax.fori_loop(0, size.row_groups, part, 0)
    for f, out in enumerate(outs):
        out[pl.ds(units * size.width, stat_rows(units)), :] = stats[f].astype(jnp.bfloat16)


def attention_part(size, far, places, lists, counts, qa, qb, keys, values, own_keys, own_values):
    units, half = size.lines, size.rows // 2
    length = units * size.width + stat_rows(units)
    count = len(places)
    chips = size.n // size.row_groups // 2
    return pl.pallas_call(
        functools.partial(attention_kernel, size, far, places),
        out_shape=[jax.ShapeDtypeStruct((length, half), jnp.bfloat16)] * count,
        in_specs=[whole(pltpu.SMEM)] * 2 + [whole()] * 6,
        out_specs=[whole()] * count,
        scratch_shapes=[
            pltpu.VMEM(
                (size.row_groups, size.cand, size.kv, chips, size.toks * size.group, size.width),
                jnp.bfloat16,
            ),
            pltpu.VMEM((size.cand, count, size.width, half), jnp.float32),
            pltpu.VMEM((size.cand, count, OWN_ROWS, half), jnp.float32),
            pltpu.VMEM((size.cand, count, 8, half), jnp.float32),
            pltpu.VMEM((size.cand, count, 8, half), jnp.float32),
            pltpu.VMEM((count, stat_rows(units), half), jnp.float32),
        ],
        compiler_params=pltpu.CompilerParams(vmem_limit_bytes=LIMIT),
        name="attention",
    )(lists, counts, qa, qb, keys, values, own_keys, own_values)


def merge_units(size, parts, at, units, unit):
    stats = []
    for ref in parts:
        block = ref[pl.ds(at, stat_rows(units)), :].astype(jnp.float32)
        m = block[unit : unit + 1]
        l = block[units + unit : units + unit + 1] + block[2 * units + unit : 2 * units + unit + 1]
        stats.append((m, l))
    high = functools.reduce(jnp.maximum, [m for m, _ in stats])
    fades = [jnp.exp2(m - high) for m, _ in stats]
    total = functools.reduce(jnp.add, [l * f for (_, l), f in zip(stats, fades)])
    sums = None
    for ref, fade in zip(parts, fades):
        value = ref[pl.ds(unit * size.width, size.width), :].astype(jnp.float32) * fade
        sums = value if sums is None else sums + value
    return sums, high, total


def split_kernel(size, count, *refs):
    near, far, outs = refs[:count], refs[count : 2 * count], refs[2 * count :]
    here = lax.axis_index("ctx") // size.kv
    lines, width = size.lines, size.width
    for unit in range(lines):
        merged = [merge_units(size, side, lines * width, lines, unit) for side in (near, far)]
        lengths = [in_bf16(total) for _, _, total in merged]
        tail = [high for _, high, _ in merged] + lengths
        tail += [total - length for (_, _, total), length in zip(merged, lengths)]
        tail.append(jnp.zeros((stat_rows(2) - len(tail), near[0].shape[1]), jnp.float32))
        tail = jnp.concatenate(tail).astype(jnp.bfloat16)
        bodies = [sums.astype(jnp.bfloat16) for sums, _, _ in merged]
        for line, out in enumerate(outs):

            @pl.when((here ^ line) == unit)
            def _():
                out[:width, :] = bodies[0]
                out[width : 2 * width, :] = bodies[1]
                out[2 * width :, :] = tail


def split_merge(size, near, far):
    shape = jax.ShapeDtypeStruct((2 * size.width + stat_rows(2), size.rows // 2), jnp.bfloat16)
    return pl.pallas_call(
        functools.partial(split_kernel, size, len(near)),
        out_shape=[shape] * size.lines,
        in_specs=[whole()] * (2 * len(near)),
        out_specs=[whole()] * size.lines,
        compiler_params=pltpu.CompilerParams(vmem_limit_bytes=LIMIT),
        name="split",
    )(*near, *far)


def finish_kernel(size, *refs):
    parts, out, turned = refs[:-2], refs[-2], refs[-1]
    chip_rows = size.toks * size.group
    spot, core = lax.axis_index("ctx") % size.kv, lax.axis_index("tp")
    b_here = (spot >> (1 - core)) & 1
    for side in range(2):
        sums, _, total = merge_units(size, parts, 2 * size.width, 2, side)
        half = (sums / total).T
        for chip in range(size.n // size.row_groups // 2):
            absolute = chip // 2 * size.kv + ((chip % 2) << core) + ((b_here ^ side) << (1 - core))
            to = pl.multiple_of(absolute * chip_rows, chip_rows)
            turned[pl.ds(to, chip_rows), :] = half[chip * chip_rows : (chip + 1) * chip_rows]
    for g in range(size.group):
        piece = turned[pl.ds(g, size.group_tokens, stride=size.group), :]
        out[pl.ds(g * size.group_tokens, size.group_tokens), :] = piece.astype(jnp.bfloat16)


def finish(size, parts):
    return pl.pallas_call(
        functools.partial(finish_kernel, size),
        out_shape=jax.ShapeDtypeStruct((size.rows, size.width), jnp.bfloat16),
        in_specs=[whole()] * len(parts),
        out_specs=whole(),
        scratch_shapes=[pltpu.VMEM((size.rows, size.width), jnp.float32)],
        compiler_params=pltpu.CompilerParams(vmem_limit_bytes=LIMIT),
        name="finish",
    )(*parts)


def project_kernel(size, a0, a1, a2, a3, weight, kept, sent, whole_rows, product):
    core = lax.axis_index("tp")
    for index, ref in enumerate((a0, a1, a2, a3)):
        for line in range(size.lines):
            chip = place(size, line, index % 2, index // 2)
            kv, other = chip % size.kv, chip // size.kv
            j, part = other % size.cand, other // size.cand
            at = pl.multiple_of(j * size.tokens + part * size.group_tokens, size.group_tokens)
            for g in range(size.group):
                piece = ref[line, pl.ds(g * size.group_tokens, size.group_tokens), :]
                whole_rows[kv * size.group + g, pl.ds(at, size.group_tokens), :] = piece
    total = None
    for h in range(0, size.heads, 2):
        pair = jnp.concatenate([whole_rows[h], whole_rows[h + 1]], axis=1)
        term = jnp.dot(
            pair,
            weight[pl.ds(h * size.width, 2 * size.width), :],
            preferred_element_type=jnp.float32,
        )
        total = term if total is None else total + term
    product[...] = total
    half = size.tokens // 2
    for j in range(size.cand):
        near = pl.multiple_of(j * size.tokens + core * half, half)
        far = pl.multiple_of(j * size.tokens + (1 - core) * half, half)
        kept[j] = product[pl.ds(near, half), :]
        sent[j] = product[pl.ds(far, half), :].astype(jnp.bfloat16)


def project(size, gathered, weight):
    columns = weight.shape[1]
    shape = (size.cand, size.tokens // 2, columns)
    return pl.pallas_call(
        functools.partial(project_kernel, size),
        out_shape=[
            jax.ShapeDtypeStruct(shape, jnp.float32),
            jax.ShapeDtypeStruct(shape, jnp.bfloat16),
        ],
        in_specs=[whole()] * 5,
        out_specs=[whole()] * 2,
        scratch_shapes=[
            pltpu.VMEM((size.heads, size.cand * size.tokens, size.width), jnp.bfloat16),
            pltpu.VMEM((size.cand * size.tokens, columns), jnp.float32),
        ],
        compiler_params=pltpu.CompilerParams(vmem_limit_bytes=LIMIT),
        name="project",
    )(*gathered, weight)


def gather_all(size, value):
    a0 = gather_lines(size, value)
    a1 = hop(size, a0, "first")
    a2 = hop(size, a0, "second")
    a3 = hop(size, a0, "both")
    return a0, a1, a2, a3


def listed_here(size, block_lists):
    lowest = lax.axis_index("ctx") * size.blocks
    local = block_lists - lowest
    below = jnp.sum((local < 0).astype(jnp.int32), axis=1)
    inside = jnp.sum((local < size.blocks).astype(jnp.int32), axis=1) - below
    slots = jnp.arange(-(-size.blocks // GROUP) * GROUP)
    entry = jnp.arange(block_lists.shape[1])
    hit = entry[None, None, :] == (below[:, None] + slots[None, :])[:, :, None]
    hit = hit & (slots[None, :] < inside[:, None])[:, :, None]
    return jnp.sum(jnp.where(hit, local[:, None, :], 0), axis=2), inside


def on_device(
    queries,
    cand_keys,
    candidate_values,
    cached_prompt_keys,
    cached_prompt_values,
    block_lists,
    out_weight,
):
    size = Sizes(
        lax.axis_size("ctx"), queries.shape, cached_prompt_keys.shape, cand_keys.shape[2]
    )
    lists, counts = listed_here(size, block_lists)
    keys = jnp.transpose(cached_prompt_keys, (2, 0, 1, 3))
    values = jnp.transpose(cached_prompt_values, (2, 0, 1, 3))
    room = ((0, 0), (0, 0), (0, OWN_ROWS - size.toks), (0, 0))
    own_keys = jnp.pad(jnp.transpose(cand_keys, (0, 2, 1, 3)), room)
    own_values = jnp.pad(jnp.transpose(candidate_values, (0, 2, 1, 3)), room)
    moved = [queries] + [hop(size, queries, k) for k in range(1, size.lines)]
    ready = (lists, counts, keys, values, own_keys, own_values)
    moved, (lists, counts, keys, values, own_keys, own_values) = lax.optimization_barrier((moved, ready))
    q0 = jnp.stack(moved)
    q1, q2 = hop(size, q0, "first"), hop(size, q0, "second")
    q3 = hop(size, q1, "second")
    shared = (keys, values, own_keys, own_values)
    lines = size.lines
    near_a, near_ab, near_b, near = attention_part(
        size, 0, ((1, 0), (1, 1), (0, 1), (0, 0)), lists, counts, q0, q1, *shared
    )
    near_a, near_ab, near_b = hop(size, near_a, "first"), hop(size, near_ab, "both"), hop(size, near_b, "second")
    far_a, far_ab = attention_part(size, 1, ((1, 0), (1, 1)), lists, counts, q2, q3, *shared)
    far_a, far_ab = hop(size, far_a, "first"), hop(size, far_ab, "both")
    far_b, far = attention_part(size, 1, ((0, 1), (0, 0)), lists, counts, q2, q3, *shared)
    far_b = hop(size, far_b, "second")
    parts = split_merge(size, (near, near_a, far_b, far_ab), (far, far_a, near_b, near_ab))
    parts = [parts[0]] + [hop(size, parts[k], k) for k in range(1, lines)]
    attention = finish(size, parts)
    kept, sent = project(size, gather_all(size, attention), out_weight)
    cores = lax.axis_size("tp")
    sent = lax.ppermute(sent, "tp", [(i, cores - 1 - i) for i in range(cores)])
    return (kept + sent.astype(jnp.float32)).astype(jnp.bfloat16)


def solution(mesh):
    placed = (
        P("groups", "ctx", "tp", None),
        P("groups", "ctx", "tp", None),
        P("groups", "ctx", "tp", None),
        P(("groups", "ctx"), None, "tp", None),
        P(("groups", "ctx"), None, "tp", None),
        P("groups", None),
        P("tp", "ctx"),
    )
    return jax.shard_map(
        on_device, mesh=mesh, in_specs=placed, out_specs=P("groups", "tp", "ctx"), check_vma=False
    )
```

```python
import functools
import math

import jax
import jax.numpy as jnp
from jax import lax
from jax.experimental import pallas as pl
from jax.experimental.pallas import tpu as pltpu
from jax.sharding import PartitionSpec as P

NEGATIVE = -1e30
POSITIVE = 1e30
STATS = 3
OWN_ROWS = 16
GROUP = 8
LIMIT = 48 * 1024 * 1024

NT = (((1,), (1,)), ((), ()))
TN = (((0,), (0,)), ((), ()))


def whole(space=pltpu.VMEM):
    return pl.BlockSpec(memory_space=space)


def in_bf16(value):
    return value.astype(jnp.bfloat16).astype(jnp.float32)


def stat_rows(units):
    return -(-units * STATS // 16) * 16


class Sizes:
    def __init__(self, ranges, queries, cached, kv):
        self.n = ranges
        self.cand, self.toks, self.heads, self.width = queries
        self.kv = kv
        self.group = self.heads // kv
        self.blocks, self.block_tokens = cached[0], cached[1]
        self.lines = ranges // kv
        self.row_groups = self.lines // self.cand
        self.tokens = self.toks * ranges
        self.group_tokens = self.tokens // self.row_groups
        self.rows = self.group_tokens * self.group
        if kv != 4 or self.row_groups * self.cand * kv != ranges:
            raise ValueError("shape")


def place(size, line, first, second):
    me, core = lax.axis_index("ctx"), lax.axis_index("tp")
    other = (me // size.kv) ^ line
    return other * size.kv + ((me % size.kv) ^ (first * (1 + core)) ^ (second * (2 - core)))


def hop(size, value, stage):
    pairs = []
    cores = lax.axis_size("tp")
    for c in range(size.n):
        for core in range(cores):
            if stage == "first":
                other = c ^ (1 + core)
            elif stage == "second":
                other = c ^ (2 - core)
            elif stage == "both":
                other = c ^ 3
            else:
                other = c ^ (stage * size.kv)
            pairs.append((c * cores + core, other * cores + core))
    return lax.ppermute(value, ("ctx", "tp"), pairs)


def gather_lines(size, value):
    return jnp.stack([value] + [hop(size, value, k) for k in range(1, size.lines)])


def attention_kernel(size, far, places, lists, counts, qa, qb, keys, values, own_keys, own_values, *rest):
    outs, (rows, acc, first_scores, tops, sums, stats) = rest[: len(places)], rest[len(places) :]
    units = size.lines
    half = size.rows // 2
    chip_rows = size.toks * size.group
    scale = size.width ** (-0.5) * math.log2(math.e)
    me, core = lax.axis_index("ctx"), lax.axis_index("tp")
    here, spot = me // size.kv, me % size.kv
    a_here = (spot >> core) & 1
    b_side = ((spot >> (1 - core)) & 1) ^ far
    for first, ref in enumerate((qa, qb)):
        for line in range(size.lines):
            other = here ^ line
            chip = (other % size.cand) * 2 + (a_here ^ first)
            for j in range(size.cand):
                parts = [ref[line, j, t].astype(jnp.float32) for t in range(size.toks)]
                for kv in range(size.kv):
                    cut = [p[kv * size.group : (kv + 1) * size.group] for p in parts]
                    rows[other // size.cand, j, kv, chip] = jnp.concatenate(cut).astype(jnp.bfloat16)
    heads = [place(size, 0, *at) % size.kv for at in places]

    def weighed(scores, live, before, own_top):
        highs = [
            jnp.where(alive, jnp.max(s.reshape(-1, 8, half), axis=0) * scale, NEGATIVE)
            for s, alive in zip(scores, live)
        ]
        if own_top is not None:
            highs.append(own_top)
        high = in_bf16(jnp.max(functools.reduce(jnp.maximum, highs), axis=0, keepdims=True))
        fade = None
        if before is not None:
            high = jnp.maximum(before, high)
            fade = jnp.exp2(before - high)
        weights, total = [], None
        for s, alive in zip(scores, live):
            p = jnp.exp2(s * scale - jnp.where(alive, high, POSITIVE))
            part = jnp.sum(p.reshape(-1, 8, half), axis=0)
            total = part if total is None else total + part
            weights.append(p.astype(jnp.bfloat16))
        return high, weights, total, fade

    def blocks_of(j, head, q, g):
        slots = [g * GROUP + b for b in range(GROUP)]
        live = [slot < counts[j] for slot in slots]
        blocks = [lists[j, slot] for slot in slots]
        scores = lax.dot_general(
            jnp.concatenate([keys[head, block] for block in blocks]),
            q,
            NT,
            preferred_element_type=jnp.float32,
        )
        scores = [scores[b * size.block_tokens : (b + 1) * size.block_tokens] for b in range(GROUP)]
        return scores, live, [values[head, block] for block in blocks]

    def gathered_values(cut, weights):
        return lax.dot_general(
            jnp.concatenate(cut), jnp.concatenate(weights), TN, preferred_element_type=jnp.float32
        )

    def part(group, carry):
        lane = lax.broadcasted_iota(jnp.int32, (OWN_ROWS, half), 1)
        chip = lane // chip_rows
        line = group * size.cand + chip // 2
        chip = line * size.kv + ((chip % 2) << core) + (b_side << (1 - core))
        token = chip * size.toks + (lane % chip_rows) // size.group
        own = lax.broadcasted_iota(jnp.int32, (OWN_ROWS, half), 0)
        seen = (own < size.toks) & (own + me * size.toks <= token)
        for j in range(size.cand):
            for h, head in enumerate(heads):
                q = rows[group, j, head].reshape(half, size.width)
                s = lax.dot_general(own_keys[j, head], q, NT, preferred_element_type=jnp.float32)
                first_scores[j, h] = jnp.where(seen, s * scale, NEGATIVE)

        work = [(j, h) for j in range(size.cand) for h in range(len(heads))]
        found = []
        for j, h in work:
            q = rows[group, j, heads[h]].reshape(half, size.width)
            found.append(blocks_of(j, heads[h], q, 0))
        for (j, h), (scores, live, cut) in zip(work, found):
            own_scores = first_scores[j, h]
            own_top = jnp.max(own_scores.reshape(-1, 8, half), axis=0)
            high, weights, total, _ = weighed(scores, live, None, own_top)
            p = jnp.where(seen, jnp.exp2(own_scores - high), 0.0)
            total = total + jnp.sum(p.reshape(-1, 8, half), axis=0)
            acc[j, h] = gathered_values(
                cut + [own_values[j, heads[h]]], weights + [p.astype(jnp.bfloat16)]
            )
            tops[j, h] = jnp.broadcast_to(high, (8, half))
            sums[j, h] = total

        def more(j, carry):
            def over(g, carry):
                found = []
                for head in heads:
                    q = rows[group, j, head].reshape(half, size.width)
                    found.append(blocks_of(j, head, q, g))
                for h, (scores, live, cut) in enumerate(found):
                    before = tops[j, h, 0:1]
                    high, weights, total, fade = weighed(scores, live, before, None)
                    acc[j, h] = acc[j, h] * fade + gathered_values(cut, weights)
                    sums[j, h] = sums[j, h] * fade + total
                    tops[j, h] = jnp.broadcast_to(high, (8, half))
                return carry

            return lax.fori_loop(1, (counts[j] + GROUP - 1) // GROUP, over, carry)

        lax.fori_loop(0, size.cand, more, 0)
        for j in range(size.cand):
            for h in range(len(heads)):
                out, unit = outs[h], group * size.cand + j
                at = pl.multiple_of(unit * size.width, size.width)
                out[pl.ds(at, size.width), :] = acc[j, h].astype(jnp.bfloat16)
                l = jnp.sum(sums[j, h], axis=0, keepdims=True)
                rounded = in_bf16(l)
                stats[h, pl.ds(unit, 1), :] = tops[j, h, 0:1]
                stats[h, pl.ds(units + unit, 1), :] = rounded
                stats[h, pl.ds(2 * units + unit, 1), :] = l - rounded
        return carry

    stats[...] = jnp.zeros_like(stats)
    lax.fori_loop(0, size.row_groups, part, 0)
    for f, out in enumerate(outs):
        out[pl.ds(units * size.width, stat_rows(units)), :] = stats[f].astype(jnp.bfloat16)


def attention_part(size, far, places, lists, counts, qa, qb, keys, values, own_keys, own_values):
    units, half = size.lines, size.rows // 2
    length = units * size.width + stat_rows(units)
    count = len(places)
    chips = size.n // size.row_groups // 2
    return pl.pallas_call(
        functools.partial(attention_kernel, size, far, places),
        out_shape=[jax.ShapeDtypeStruct((length, half), jnp.bfloat16)] * count,
        in_specs=[whole(pltpu.SMEM)] * 2 + [whole()] * 6,
        out_specs=[whole()] * count,
        scratch_shapes=[
            pltpu.VMEM(
                (size.row_groups, size.cand, size.kv, chips, size.toks * size.group, size.width),
                jnp.bfloat16,
            ),
            pltpu.VMEM((size.cand, count, size.width, half), jnp.float32),
            pltpu.VMEM((size.cand, count, OWN_ROWS, half), jnp.float32),
            pltpu.VMEM((size.cand, count, 8, half), jnp.float32),
            pltpu.VMEM((size.cand, count, 8, half), jnp.float32),
            pltpu.VMEM((count, stat_rows(units), half), jnp.float32),
        ],
        compiler_params=pltpu.CompilerParams(vmem_limit_bytes=LIMIT),
        name="attention",
    )(lists, counts, qa, qb, keys, values, own_keys, own_values)


def merge_units(size, parts, at, units, unit):
    stats = []
    for ref in parts:
        block = ref[pl.ds(at, stat_rows(units)), :].astype(jnp.float32)
        m = block[unit : unit + 1]
        l = block[units + unit : units + unit + 1] + block[2 * units + unit : 2 * units + unit + 1]
        stats.append((m, l))
    high = functools.reduce(jnp.maximum, [m for m, _ in stats])
    fades = [jnp.exp2(m - high) for m, _ in stats]
    total = functools.reduce(jnp.add, [l * f for (_, l), f in zip(stats, fades)])
    sums = None
    for ref, fade in zip(parts, fades):
        value = ref[pl.ds(unit * size.width, size.width), :].astype(jnp.float32) * fade
        sums = value if sums is None else sums + value
    return sums, high, total


def split_kernel(size, count, *refs):
    near, far, outs = refs[:count], refs[count : 2 * count], refs[2 * count :]
    here = lax.axis_index("ctx") // size.kv
    lines, width = size.lines, size.width
    for unit in range(lines):
        merged = [merge_units(size, side, lines * width, lines, unit) for side in (near, far)]
        lengths = [in_bf16(total) for _, _, total in merged]
        tail = [high for _, high, _ in merged] + lengths
        tail += [total - length for (_, _, total), length in zip(merged, lengths)]
        tail.append(jnp.zeros((stat_rows(2) - len(tail), near[0].shape[1]), jnp.float32))
        tail = jnp.concatenate(tail).astype(jnp.bfloat16)
        bodies = [sums.astype(jnp.bfloat16) for sums, _, _ in merged]
        for line, out in enumerate(outs):

            @pl.when((here ^ line) == unit)
            def _():
                out[:width, :] = bodies[0]
                out[width : 2 * width, :] = bodies[1]
                out[2 * width :, :] = tail


def split_merge(size, near, far):
    shape = jax.ShapeDtypeStruct((2 * size.width + stat_rows(2), size.rows // 2), jnp.bfloat16)
    return pl.pallas_call(
        functools.partial(split_kernel, size, len(near)),
        out_shape=[shape] * size.lines,
        in_specs=[whole()] * (2 * len(near)),
        out_specs=[whole()] * size.lines,
        compiler_params=pltpu.CompilerParams(vmem_limit_bytes=LIMIT),
        name="split",
    )(*near, *far)


def finish_kernel(size, *refs):
    parts, out, turned = refs[:-2], refs[-2], refs[-1]
    chip_rows = size.toks * size.group
    spot, core = lax.axis_index("ctx") % size.kv, lax.axis_index("tp")
    b_here = (spot >> (1 - core)) & 1
    for side in range(2):
        sums, _, total = merge_units(size, parts, 2 * size.width, 2, side)
        half = (sums / total).T
        for chip in range(size.n // size.row_groups // 2):
            absolute = chip // 2 * size.kv + ((chip % 2) << core) + ((b_here ^ side) << (1 - core))
            to = pl.multiple_of(absolute * chip_rows, chip_rows)
            turned[pl.ds(to, chip_rows), :] = half[chip * chip_rows : (chip + 1) * chip_rows]
    for g in range(size.group):
        piece = turned[pl.ds(g, size.group_tokens, stride=size.group), :]
        out[pl.ds(g * size.group_tokens, size.group_tokens), :] = piece.astype(jnp.bfloat16)


def finish(size, parts):
    return pl.pallas_call(
        functools.partial(finish_kernel, size),
        out_shape=jax.ShapeDtypeStruct((size.rows, size.width), jnp.bfloat16),
        in_specs=[whole()] * len(parts),
        out_specs=whole(),
        scratch_shapes=[pltpu.VMEM((size.rows, size.width), jnp.float32)],
        compiler_params=pltpu.CompilerParams(vmem_limit_bytes=LIMIT),
        name="finish",
    )(*parts)


def project_kernel(size, a0, a1, a2, a3, weight, kept, sent, whole_rows, product):
    core = lax.axis_index("tp")
    for index, ref in enumerate((a0, a1, a2, a3)):
        for line in range(size.lines):
            chip = place(size, line, index % 2, index // 2)
            kv, other = chip % size.kv, chip // size.kv
            j, part = other % size.cand, other // size.cand
            at = pl.multiple_of(j * size.tokens + part * size.group_tokens, size.group_tokens)
            for g in range(size.group):
                piece = ref[line, pl.ds(g * size.group_tokens, size.group_tokens), :]
                whole_rows[kv * size.group + g, pl.ds(at, size.group_tokens), :] = piece
    total = None
    for h in range(0, size.heads, 2):
        pair = jnp.concatenate([whole_rows[h], whole_rows[h + 1]], axis=1)
        term = jnp.dot(
            pair,
            weight[pl.ds(h * size.width, 2 * size.width), :],
            preferred_element_type=jnp.float32,
        )
        total = term if total is None else total + term
    product[...] = total
    half = size.tokens // 2
    for j in range(size.cand):
        near = pl.multiple_of(j * size.tokens + core * half, half)
        far = pl.multiple_of(j * size.tokens + (1 - core) * half, half)
        kept[j] = product[pl.ds(near, half), :]
        sent[j] = product[pl.ds(far, half), :].astype(jnp.bfloat16)


def project(size, gathered, weight):
    columns = weight.shape[1]
    shape = (size.cand, size.tokens // 2, columns)
    return pl.pallas_call(
        functools.partial(project_kernel, size),
        out_shape=[
            jax.ShapeDtypeStruct(shape, jnp.float32),
            jax.ShapeDtypeStruct(shape, jnp.bfloat16),
        ],
        in_specs=[whole()] * 5,
        out_specs=[whole()] * 2,
        scratch_shapes=[
            pltpu.VMEM((size.heads, size.cand * size.tokens, size.width), jnp.bfloat16),
            pltpu.VMEM((size.cand * size.tokens, columns), jnp.float32),
        ],
        compiler_params=pltpu.CompilerParams(vmem_limit_bytes=LIMIT),
        name="project",
    )(*gathered, weight)


def gather_all(size, value):
    a0 = gather_lines(size, value)
    a1 = hop(size, a0, "first")
    a2 = hop(size, a0, "second")
    a3 = hop(size, a0, "both")
    return a0, a1, a2, a3


def listed_here(size, block_lists):
    lowest = lax.axis_index("ctx") * size.blocks
    local = block_lists - lowest
    below = jnp.sum((local < 0).astype(jnp.int32), axis=1)
    inside = jnp.sum((local < size.blocks).astype(jnp.int32), axis=1) - below
    slots = jnp.arange(-(-size.blocks // GROUP) * GROUP)
    entry = jnp.arange(block_lists.shape[1])
    hit = entry[None, None, :] == (below[:, None] + slots[None, :])[:, :, None]
    hit = hit & (slots[None, :] < inside[:, None])[:, :, None]
    return jnp.sum(jnp.where(hit, local[:, None, :], 0), axis=2), inside


def on_device(
    queries,
    cand_keys,
    candidate_values,
    cached_prompt_keys,
    cached_prompt_values,
    block_lists,
    out_weight,
):
    size = Sizes(
        lax.axis_size("ctx"), queries.shape, cached_prompt_keys.shape, cand_keys.shape[2]
    )
    lists, counts = listed_here(size, block_lists)
    keys = jnp.transpose(cached_prompt_keys, (2, 0, 1, 3))
    values = jnp.transpose(cached_prompt_values, (2, 0, 1, 3))
    room = ((0, 0), (0, 0), (0, OWN_ROWS - size.toks), (0, 0))
    own_keys = jnp.pad(jnp.transpose(cand_keys, (0, 2, 1, 3)), room)
    own_values = jnp.pad(jnp.transpose(candidate_values, (0, 2, 1, 3)), room)
    moved = [queries] + [hop(size, queries, k) for k in range(1, size.lines)]
    ready = (lists, counts, keys, values, own_keys, own_values)
    moved, (lists, counts, keys, values, own_keys, own_values) = lax.optimization_barrier((moved, ready))
    q0 = jnp.stack(moved)
    q1, q2 = hop(size, q0, "first"), hop(size, q0, "second")
    q3 = hop(size, q1, "second")
    shared = (keys, values, own_keys, own_values)
    lines = size.lines
    near_a, near_ab, near_b, near = attention_part(
        size, 0, ((1, 0), (1, 1), (0, 1), (0, 0)), lists, counts, q0, q1, *shared
    )
    near_a, near_ab, near_b = hop(size, near_a, "first"), hop(size, near_ab, "both"), hop(size, near_b, "second")
    far_a, far_ab, far_b, far = attention_part(
        size, 1, ((1, 0), (1, 1), (0, 1), (0, 0)), lists, counts, q2, q3, *shared
    )
    far_a, far_ab, far_b = hop(size, far_a, "first"), hop(size, far_ab, "both"), hop(size, far_b, "second")
    parts = split_merge(size, (near, near_a, far_b, far_ab), (far, far_a, near_b, near_ab))
    parts = [parts[0]] + [hop(size, parts[k], k) for k in range(1, lines)]
    attention = finish(size, parts)
    kept, sent = project(size, gather_all(size, attention), out_weight)
    cores = lax.axis_size("tp")
    sent = lax.ppermute(sent, "tp", [(i, cores - 1 - i) for i in range(cores)])
    return (kept + sent.astype(jnp.float32)).astype(jnp.bfloat16)


def solution(mesh):
    placed = (
        P("groups", "ctx", "tp", None),
        P("groups", "ctx", "tp", None),
        P("groups", "ctx", "tp", None),
        P(("groups", "ctx"), None, "tp", None),
        P(("groups", "ctx"), None, "tp", None),
        P("groups", None),
        P("tp", "ctx"),
    )
    return jax.shard_map(
        on_device, mesh=mesh, in_specs=placed, out_specs=P("groups", "tp", "ctx"), check_vma=False
    )
```

```python
import functools
import math

import jax
import jax.numpy as jnp
from jax import lax
from jax.experimental import pallas as pl
from jax.experimental.pallas import tpu as pltpu
from jax.sharding import PartitionSpec as P

NEGATIVE = -1e30
POSITIVE = 1e30
STATS = 3
OWN_ROWS = 16
GROUP = 8
LIMIT = 48 * 1024 * 1024

NT = (((1,), (1,)), ((), ()))
TN = (((0,), (0,)), ((), ()))


def whole(space=pltpu.VMEM):
    return pl.BlockSpec(memory_space=space)


def in_bf16(value):
    return value.astype(jnp.bfloat16).astype(jnp.float32)


def stat_rows(units):
    return -(-units * STATS // 16) * 16


class Sizes:
    def __init__(self, ranges, queries, cached, kv):
        self.n = ranges
        self.cand, self.toks, self.heads, self.width = queries
        self.kv = kv
        self.group = self.heads // kv
        self.blocks, self.block_tokens = cached[0], cached[1]
        self.lines = ranges // kv
        self.row_groups = self.lines // self.cand
        self.tokens = self.toks * ranges
        self.group_tokens = self.tokens // self.row_groups
        self.rows = self.group_tokens * self.group
        if kv != 4 or self.row_groups * self.cand * kv != ranges:
            raise ValueError("shape")


def place(size, line, first, second):
    me, core = lax.axis_index("ctx"), lax.axis_index("tp")
    other = (me // size.kv) ^ line
    return other * size.kv + ((me % size.kv) ^ (first * (1 + core)) ^ (second * (2 - core)))


def hop(size, value, stage):
    pairs = []
    cores = lax.axis_size("tp")
    for c in range(size.n):
        for core in range(cores):
            if stage == "first":
                other = c ^ (1 + core)
            elif stage == "second":
                other = c ^ (2 - core)
            elif stage == "both":
                other = c ^ 3
            else:
                other = c ^ (stage * size.kv)
            pairs.append((c * cores + core, other * cores + core))
    return lax.ppermute(value, ("ctx", "tp"), pairs)


def gather_lines(size, value):
    return jnp.stack([value] + [hop(size, value, k) for k in range(1, size.lines)])


def attention_kernel(size, far, places, lists, counts, qa, qb, keys, values, own_keys, own_values, *rest):
    outs, (rows, acc, first_scores, tops, sums, stats) = rest[: len(places)], rest[len(places) :]
    units = size.lines
    half = size.rows // 2
    chip_rows = size.toks * size.group
    scale = size.width ** (-0.5) * math.log2(math.e)
    me, core = lax.axis_index("ctx"), lax.axis_index("tp")
    here, spot = me // size.kv, me % size.kv
    a_here = (spot >> core) & 1
    b_side = ((spot >> (1 - core)) & 1) ^ far
    for first, ref in enumerate((qa, qb)):
        for line in range(size.lines):
            other = here ^ line
            chip = (other % size.cand) * 2 + (a_here ^ first)
            for j in range(size.cand):
                parts = [ref[line, j, t].astype(jnp.float32) for t in range(size.toks)]
                for kv in range(size.kv):
                    cut = [p[kv * size.group : (kv + 1) * size.group] for p in parts]
                    rows[other // size.cand, j, kv, chip] = jnp.concatenate(cut).astype(jnp.bfloat16)
    heads = [place(size, 0, *at) % size.kv for at in places]

    def weighed(scores, live, before, own_top):
        highs = [
            jnp.where(alive, jnp.max(s.reshape(-1, 8, half), axis=0) * scale, NEGATIVE)
            for s, alive in zip(scores, live)
        ]
        if own_top is not None:
            highs.append(own_top)
        high = in_bf16(jnp.max(functools.reduce(jnp.maximum, highs), axis=0, keepdims=True))
        fade = None
        if before is not None:
            high = jnp.maximum(before, high)
            fade = jnp.exp2(before - high)
        weights, total = [], None
        for s, alive in zip(scores, live):
            p = jnp.exp2(s * scale - jnp.where(alive, high, POSITIVE))
            part = jnp.sum(p.reshape(-1, 8, half), axis=0)
            total = part if total is None else total + part
            weights.append(p.astype(jnp.bfloat16))
        return high, weights, total, fade

    def blocks_of(j, head, q, g):
        slots = [g * GROUP + b for b in range(GROUP)]
        live = [slot < counts[j] for slot in slots]
        blocks = [lists[j, slot] for slot in slots]
        scores = lax.dot_general(
            jnp.concatenate([keys[head, block] for block in blocks]),
            q,
            NT,
            preferred_element_type=jnp.float32,
        )
        scores = [scores[b * size.block_tokens : (b + 1) * size.block_tokens] for b in range(GROUP)]
        return scores, live, [values[head, block] for block in blocks]

    def gathered_values(cut, weights):
        return lax.dot_general(
            jnp.concatenate(cut), jnp.concatenate(weights), TN, preferred_element_type=jnp.float32
        )

    def part(group, carry):
        lane = lax.broadcasted_iota(jnp.int32, (OWN_ROWS, half), 1)
        chip = lane // chip_rows
        line = group * size.cand + chip // 2
        chip = line * size.kv + ((chip % 2) << core) + (b_side << (1 - core))
        token = chip * size.toks + (lane % chip_rows) // size.group
        own = lax.broadcasted_iota(jnp.int32, (OWN_ROWS, half), 0)
        seen = (own < size.toks) & (own + me * size.toks <= token)
        for j in range(size.cand):
            for h, head in enumerate(heads):
                q = rows[group, j, head].reshape(half, size.width)
                s = lax.dot_general(own_keys[j, head], q, NT, preferred_element_type=jnp.float32)
                first_scores[j, h] = jnp.where(seen, s * scale, NEGATIVE)

        work = [(j, h) for j in range(size.cand) for h in range(len(heads))]
        found = []
        for j, h in work:
            q = rows[group, j, heads[h]].reshape(half, size.width)
            found.append(blocks_of(j, heads[h], q, 0))
        for (j, h), (scores, live, cut) in zip(work, found):
            own_scores = first_scores[j, h]
            own_top = jnp.max(own_scores.reshape(-1, 8, half), axis=0)
            high, weights, total, _ = weighed(scores, live, None, own_top)
            p = jnp.where(seen, jnp.exp2(own_scores - high), 0.0)
            total = total + jnp.sum(p.reshape(-1, 8, half), axis=0)
            acc[j, h] = gathered_values(
                cut + [own_values[j, heads[h]]], weights + [p.astype(jnp.bfloat16)]
            )
            tops[j, h] = jnp.broadcast_to(high, (8, half))
            sums[j, h] = total

        def more(j, carry):
            def over(g, carry):
                found = []
                for head in heads:
                    q = rows[group, j, head].reshape(half, size.width)
                    found.append(blocks_of(j, head, q, g))
                for h, (scores, live, cut) in enumerate(found):
                    before = tops[j, h, 0:1]
                    high, weights, total, fade = weighed(scores, live, before, None)
                    acc[j, h] = acc[j, h] * fade + gathered_values(cut, weights)
                    sums[j, h] = sums[j, h] * fade + total
                    tops[j, h] = jnp.broadcast_to(high, (8, half))
                return carry

            return lax.fori_loop(1, (counts[j] + GROUP - 1) // GROUP, over, carry)

        lax.fori_loop(0, size.cand, more, 0)
        for j in range(size.cand):
            for h in range(len(heads)):
                out, unit = outs[h], group * size.cand + j
                at = pl.multiple_of(unit * size.width, size.width)
                out[pl.ds(at, size.width), :] = acc[j, h].astype(jnp.bfloat16)
                l = jnp.sum(sums[j, h], axis=0, keepdims=True)
                rounded = in_bf16(l)
                stats[h, pl.ds(unit, 1), :] = tops[j, h, 0:1]
                stats[h, pl.ds(units + unit, 1), :] = rounded
                stats[h, pl.ds(2 * units + unit, 1), :] = l - rounded
        return carry

    stats[...] = jnp.zeros_like(stats)
    lax.fori_loop(0, size.row_groups, part, 0)
    for f, out in enumerate(outs):
        out[pl.ds(units * size.width, stat_rows(units)), :] = stats[f].astype(jnp.bfloat16)


def attention_part(size, far, places, lists, counts, qa, qb, keys, values, own_keys, own_values):
    units, half = size.lines, size.rows // 2
    length = units * size.width + stat_rows(units)
    count = len(places)
    chips = size.n // size.row_groups // 2
    return pl.pallas_call(
        functools.partial(attention_kernel, size, far, places),
        out_shape=[jax.ShapeDtypeStruct((length, half), jnp.bfloat16)] * count,
        in_specs=[whole(pltpu.SMEM)] * 2 + [whole()] * 6,
        out_specs=[whole()] * count,
        scratch_shapes=[
            pltpu.VMEM(
                (size.row_groups, size.cand, size.kv, chips, size.toks * size.group, size.width),
                jnp.bfloat16,
            ),
            pltpu.VMEM((size.cand, count, size.width, half), jnp.float32),
            pltpu.VMEM((size.cand, count, OWN_ROWS, half), jnp.float32),
            pltpu.VMEM((size.cand, count, 8, half), jnp.float32),
            pltpu.VMEM((size.cand, count, 8, half), jnp.float32),
            pltpu.VMEM((count, stat_rows(units), half), jnp.float32),
        ],
        compiler_params=pltpu.CompilerParams(vmem_limit_bytes=LIMIT),
        name="attention",
    )(lists, counts, qa, qb, keys, values, own_keys, own_values)


def merge_units(size, parts, at, units, unit):
    stats = []
    for ref in parts:
        block = ref[pl.ds(at, stat_rows(units)), :].astype(jnp.float32)
        m = block[unit : unit + 1]
        l = block[units + unit : units + unit + 1] + block[2 * units + unit : 2 * units + unit + 1]
        stats.append((m, l))
    high = functools.reduce(jnp.maximum, [m for m, _ in stats])
    fades = [jnp.exp2(m - high) for m, _ in stats]
    total = functools.reduce(jnp.add, [l * f for (_, l), f in zip(stats, fades)])
    sums = None
    for ref, fade in zip(parts, fades):
        value = ref[pl.ds(unit * size.width, size.width), :].astype(jnp.float32) * fade
        sums = value if sums is None else sums + value
    return sums, high, total


def split_kernel(size, count, *refs):
    near, far, outs = refs[:count], refs[count : 2 * count], refs[2 * count :]
    here = lax.axis_index("ctx") // size.kv
    lines, width = size.lines, size.width
    for unit in range(lines):
        merged = [merge_units(size, side, lines * width, lines, unit) for side in (near, far)]
        lengths = [in_bf16(total) for _, _, total in merged]
        tail = [high for _, high, _ in merged] + lengths
        tail += [total - length for (_, _, total), length in zip(merged, lengths)]
        tail.append(jnp.zeros((stat_rows(2) - len(tail), near[0].shape[1]), jnp.float32))
        tail = jnp.concatenate(tail).astype(jnp.bfloat16)
        bodies = [sums.astype(jnp.bfloat16) for sums, _, _ in merged]
        for line, out in enumerate(outs):

            @pl.when((here ^ line) == unit)
            def _():
                out[:width, :] = bodies[0]
                out[width : 2 * width, :] = bodies[1]
                out[2 * width :, :] = tail


def split_merge(size, near, far):
    shape = jax.ShapeDtypeStruct((2 * size.width + stat_rows(2), size.rows // 2), jnp.bfloat16)
    return pl.pallas_call(
        functools.partial(split_kernel, size, len(near)),
        out_shape=[shape] * size.lines,
        in_specs=[whole()] * (2 * len(near)),
        out_specs=[whole()] * size.lines,
        compiler_params=pltpu.CompilerParams(vmem_limit_bytes=LIMIT),
        name="split",
    )(*near, *far)


def finish_kernel(size, *refs):
    parts, out, turned = refs[:-2], refs[-2], refs[-1]
    chip_rows = size.toks * size.group
    spot, core = lax.axis_index("ctx") % size.kv, lax.axis_index("tp")
    b_here = (spot >> (1 - core)) & 1
    for side in range(2):
        sums, _, total = merge_units(size, parts, 2 * size.width, 2, side)
        half = (sums / total).T
        for chip in range(size.n // size.row_groups // 2):
            absolute = chip // 2 * size.kv + ((chip % 2) << core) + ((b_here ^ side) << (1 - core))
            to = pl.multiple_of(absolute * chip_rows, chip_rows)
            turned[pl.ds(to, chip_rows), :] = half[chip * chip_rows : (chip + 1) * chip_rows]
    for g in range(size.group):
        piece = turned[pl.ds(g, size.group_tokens, stride=size.group), :]
        out[pl.ds(g * size.group_tokens, size.group_tokens), :] = piece.astype(jnp.bfloat16)


def finish(size, parts):
    return pl.pallas_call(
        functools.partial(finish_kernel, size),
        out_shape=jax.ShapeDtypeStruct((size.rows, size.width), jnp.bfloat16),
        in_specs=[whole()] * len(parts),
        out_specs=whole(),
        scratch_shapes=[pltpu.VMEM((size.rows, size.width), jnp.float32)],
        compiler_params=pltpu.CompilerParams(vmem_limit_bytes=LIMIT),
        name="finish",
    )(*parts)


def project_kernel(size, other, a0, a1, a2, a3, weight, out, whole_rows):
    side = lax.axis_index("tp") ^ other
    half = size.tokens // 2
    for index, ref in enumerate((a0, a1, a2, a3)):
        for line in range(size.lines):
            chip = place(size, line, index % 2, index // 2)
            kv, other = chip % size.kv, chip // size.kv
            j, part = other % size.cand, other // size.cand
            at = pl.multiple_of(j * size.tokens + part * size.group_tokens, size.group_tokens)
            for g in range(size.group):
                piece = ref[line, pl.ds(g * size.group_tokens, size.group_tokens), :]
                whole_rows[kv * size.group + g, pl.ds(at, size.group_tokens), :] = piece
    total = None
    for h in range(0, size.heads, 2):
        pair = jnp.concatenate(
            [
                jnp.concatenate(
                    [
                        whole_rows[k, pl.ds(pl.multiple_of(j * size.tokens + side * half, half), half), :]
                        for j in range(size.cand)
                    ]
                )
                for k in (h, h + 1)
            ],
            axis=1,
        )
        term = jnp.dot(
            pair,
            weight[pl.ds(h * size.width, 2 * size.width), :],
            preferred_element_type=jnp.float32,
        )
        total = term if total is None else total + term
    for j in range(size.cand):
        out[j] = total[j * half : (j + 1) * half].astype(out.dtype)


def project(size, other, dtype, gathered, weight):
    columns = weight.shape[1]
    return pl.pallas_call(
        functools.partial(project_kernel, size, other),
        out_shape=jax.ShapeDtypeStruct((size.cand, size.tokens // 2, columns), dtype),
        in_specs=[whole()] * 5,
        out_specs=whole(),
        scratch_shapes=[
            pltpu.VMEM((size.heads, size.cand * size.tokens, size.width), jnp.bfloat16),
        ],
        compiler_params=pltpu.CompilerParams(vmem_limit_bytes=LIMIT),
        name="project",
    )(*gathered, weight)


def gather_all(size, value):
    a0 = gather_lines(size, value)
    a1 = hop(size, a0, "first")
    a2 = hop(size, a0, "second")
    a3 = hop(size, a0, "both")
    return a0, a1, a2, a3


def listed_here(size, block_lists):
    lowest = lax.axis_index("ctx") * size.blocks
    local = block_lists - lowest
    below = jnp.sum((local < 0).astype(jnp.int32), axis=1)
    inside = jnp.sum((local < size.blocks).astype(jnp.int32), axis=1) - below
    slots = jnp.arange(-(-size.blocks // GROUP) * GROUP)
    entry = jnp.arange(block_lists.shape[1])
    hit = entry[None, None, :] == (below[:, None] + slots[None, :])[:, :, None]
    hit = hit & (slots[None, :] < inside[:, None])[:, :, None]
    return jnp.sum(jnp.where(hit, local[:, None, :], 0), axis=2), inside


def on_device(
    queries,
    cand_keys,
    candidate_values,
    cached_prompt_keys,
    cached_prompt_values,
    block_lists,
    out_weight,
):
    size = Sizes(
        lax.axis_size("ctx"), queries.shape, cached_prompt_keys.shape, cand_keys.shape[2]
    )
    lists, counts = listed_here(size, block_lists)
    keys = jnp.transpose(cached_prompt_keys, (2, 0, 1, 3))
    values = jnp.transpose(cached_prompt_values, (2, 0, 1, 3))
    room = ((0, 0), (0, 0), (0, OWN_ROWS - size.toks), (0, 0))
    own_keys = jnp.pad(jnp.transpose(cand_keys, (0, 2, 1, 3)), room)
    own_values = jnp.pad(jnp.transpose(candidate_values, (0, 2, 1, 3)), room)
    moved = [queries] + [hop(size, queries, k) for k in range(1, size.lines)]
    ready = (lists, counts, keys, values, own_keys, own_values)
    moved, (lists, counts, keys, values, own_keys, own_values) = lax.optimization_barrier((moved, ready))
    q0 = jnp.stack(moved)
    q1, q2 = hop(size, q0, "first"), hop(size, q0, "second")
    q3 = hop(size, q1, "second")
    shared = (keys, values, own_keys, own_values)
    lines = size.lines
    near_a, near_ab, near_b, near = attention_part(
        size, 0, ((1, 0), (1, 1), (0, 1), (0, 0)), lists, counts, q0, q1, *shared
    )
    near_a, near_ab, near_b = hop(size, near_a, "first"), hop(size, near_ab, "both"), hop(size, near_b, "second")
    far_a, far_ab, far_b, far = attention_part(
        size, 1, ((1, 0), (1, 1), (0, 1), (0, 0)), lists, counts, q2, q3, *shared
    )
    far_a, far_ab, far_b = hop(size, far_a, "first"), hop(size, far_ab, "both"), hop(size, far_b, "second")
    parts = split_merge(size, (near, near_a, far_b, far_ab), (far, far_a, near_b, near_ab))
    parts = [parts[0]] + [hop(size, parts[k], k) for k in range(1, lines)]
    attention = finish(size, parts)
    gathered = gather_all(size, attention)
    sent = project(size, 1, jnp.bfloat16, gathered, out_weight)
    kept = project(size, 0, jnp.float32, gathered, out_weight)
    cores = lax.axis_size("tp")
    sent = lax.ppermute(sent, "tp", [(i, cores - 1 - i) for i in range(cores)])
    return (kept + sent.astype(jnp.float32)).astype(jnp.bfloat16)


def solution(mesh):
    placed = (
        P("groups", "ctx", "tp", None),
        P("groups", "ctx", "tp", None),
        P("groups", "ctx", "tp", None),
        P(("groups", "ctx"), None, "tp", None),
        P(("groups", "ctx"), None, "tp", None),
        P("groups", None),
        P("tp", "ctx"),
    )
    return jax.shard_map(
        on_device, mesh=mesh, in_specs=placed, out_specs=P("groups", "tp", "ctx"), check_vma=False
    )
```
